128 devices in a mesh: front: 8 (over z, x_lo), row: 8 (over x_hi, y), col: 2 (over core).
Axes of the slice: x: 4 (x_hi: 2, x_lo: 2; x = x_hi * 2 + x_lo), y: 4, z: 4, core: 2. Of those that a mesh axis runs over, the one named last changes fastest.
Arguments:
- front_matrix: float32 [8, 12, 1024, 3072], P('front', None, 'row', 'col')
- front_sizes: int32 [8], P('front'), may hold values from 8192 to 12288, as said below
- contrib: float32 [8, 4, 1024, 3072], P('front', None, 'row', 'col'), may hold values from -6 to 6
- dest_front: int32 [8, 4, 8], P('front', None, 'row'), may hold values from 0 to 7, as said below
- dest_local: int32 [8, 4, 8], P('front', None, 'row'), may hold values from 1 to 11, as said below
Outputs:
- factored: float32 [8, 12, 1024, 3072], P('front', None, 'row', 'col')
The draws below stay inside these ranges and needn't reach their ends.
Inputs may be any that keep to these rules, and one draw needn't show every extreme that they name: `front_sizes`: multiples of 128; every draw has a front of order 12288 and one of order 8192. For each (g, r), the 4 entries dest_front[g, :, r] name distinct fronts. The block (g, k, r) lands on parent rows from (dest_local * 8 + r) * 128: at or after row 1024 and wholly below the parent's order; several blocks may land on the same rows; in every draw some block lands in the last round of blocks of the largest front.
All inputs are finite; a program needn't handle non-finite values.
Results may differ from the reference program's by a relative error of at most 0.0003.
Values sent between devices are 32-bit elements; how exact they have to be, the bound alone decides.
A program may use at most 128 MiB of HBM per device.

```python
import jax
import jax.numpy as jnp
from jax import lax

FMAX = 12288
FMIN = 8192
PW = 512
BLK = 128
NPANEL = 2
KB = 4
FRONTS = 8
CYCLE = 1024
LOCB = 12
W = 3072


def rank_of_fronts(key):
    size_key = jax.random.fold_in(key, 7)
    first_key, rank_key = jax.random.split(size_key)
    return (first_key, jax.random.permutation(rank_key, FRONTS))


def layout_sizes(key):
    first_key, rank_order = rank_of_fronts(key)
    steps_count = (FMAX - FMIN) // BLK
    size_list = FMIN + BLK * jax.random.randint(first_key, (FRONTS,), 0, steps_count + 1, dtype=jnp.int32)
    size_list = jnp.where(rank_order == 0, FMAX, size_list)
    size_list = jnp.where(rank_order == 1, FMIN, size_list)
    return size_list.astype(jnp.int32)


def shuffled_fronts(one_key):
    return jax.random.permutation(one_key, FRONTS)


def layout_targets(key):
    row_count = CYCLE // BLK
    first_key, rank_order = rank_of_fronts(key)
    front_ids = jnp.arange(FRONTS, dtype=jnp.int32)
    largest = jnp.sum(jnp.where(rank_order == 0, front_ids, 0)).astype(jnp.int32)
    route_key = jax.random.fold_in(key, 8)
    route_keys = jax.random.split(route_key, FRONTS * row_count)
    orders = jax.vmap(shuffled_fronts)(route_keys).astype(jnp.int32)
    first_order = orders[0]
    leading = first_order[0]
    fixed_order = jnp.where(front_ids == 0, largest, jnp.where(first_order == largest, leading, first_order))
    orders = orders.at[0].set(fixed_order)
    chosen = orders[:, :KB].reshape(FRONTS, row_count, KB)
    return jnp.transpose(chosen, (0, 2, 1)).astype(jnp.int32)


def draw_front_sizes(key, part):
    return layout_sizes(key)


def draw_dest_front(key, part):
    return layout_targets(key)


def draw_dest_local(key, part):
    row_count = CYCLE // BLK
    size_list = layout_sizes(key)
    targets = layout_targets(key)
    parent = size_list[targets]
    row_index = jnp.arange(row_count, dtype=jnp.int32)[None, None, :]
    lowest = jnp.maximum(0, (NPANEL * PW // BLK - row_index + row_count - 1) // row_count)
    highest = (parent // BLK - 1 - row_index) // row_count
    local_key = jax.random.fold_in(key, 9)
    lowest = jnp.broadcast_to(lowest, (FRONTS, KB, row_count))
    drawn = jax.random.randint(local_key, (FRONTS, KB, row_count), lowest, highest + 1, dtype=jnp.int32)
    first_slot = (jnp.arange(FRONTS)[:, None, None] == 0) & (jnp.arange(KB)[None, :, None] == 0) & (jnp.arange(row_count)[None, None, :] == 0)
    return jnp.where(first_slot, highest, drawn).astype(jnp.int32)


def draw_front_matrix(key, part):
    full_shape = (FRONTS, LOCB, CYCLE, W)
    normal_key, level_key = jax.random.split(key)
    entries = jax.random.normal(normal_key, full_shape, jnp.float32)
    global_row = jnp.arange(LOCB)[:, None] * CYCLE + jnp.arange(CYCLE)[None, :]
    on_diagonal = global_row[:, :, None] == jnp.arange(W)[None, None, :]
    diagonal_level = jax.random.uniform(level_key, full_shape, jnp.float32, 96.0, 192.0)
    return jnp.where(on_diagonal[None], diagonal_level, entries)


def block_scale(own_key, dims, shards, smallest, high):
    gain = 1.0
    for position, parts in shards:
        draws = jax.random.uniform(jax.random.fold_in(jax.random.fold_in(own_key, 6), position), (parts,), jnp.float32, smallest / len(shards), high / len(shards))
        gain = gain * jnp.repeat(jnp.exp(draws), dims[position] // parts).reshape((-1,) + (1,) * (len(dims) - 1 - position))
    return gain


def bell_draw(stream_key, shape, spread, reach, pieces=(), held_as=jnp.bfloat16):
    values = jax.random.normal(stream_key, shape, jnp.float32) * spread
    if len(pieces) > 0:
        values = block_scale(stream_key, shape, pieces, -0.22, 0.18) * values
    return jnp.clip(values, min=-reach, max=reach).astype(held_as)


def setup_inputs(seed: int = 0) -> dict:
    seeds = jax.random.split(jax.random.key(seed), 6)
    return {
        "front_matrix": draw_front_matrix(jax.random.fold_in(seeds[5], 71), 0),
        "front_sizes": draw_front_sizes(jax.random.fold_in(seeds[5], 71), 0),
        "contrib": bell_draw(seeds[2], (FRONTS, KB, CYCLE, W), 1.0, 6.0, ((0, 8), (2, 8), (3, 2)), jnp.float32),
        "dest_front": draw_dest_front(jax.random.fold_in(seeds[5], 71), 0),
        "dest_local": draw_dest_local(jax.random.fold_in(seeds[5], 71), 0),
    }


def lower_inverse(pivot_block):
    symmetric = jnp.tril(pivot_block) + jnp.tril(pivot_block, -1).T
    factor = jnp.linalg.cholesky(symmetric)
    eye_block = jnp.eye(factor.shape[0], dtype=factor.dtype)
    inverse = jax.scipy.linalg.solve_triangular(factor, eye_block, lower=True)
    return (factor, inverse)

def factor_front(front_rows):
    global_row = jnp.arange(FMAX, dtype=jnp.int32)
    for panel_index in range(NPANEL):
        col_start = panel_index * PW
        factor, inverse = lower_inverse(front_rows[col_start:col_start + PW, col_start:col_start + PW])
        solved = jnp.dot(front_rows[:, col_start:col_start + PW], inverse.T, precision=lax.Precision.HIGHEST)
        solved = jnp.where((global_row < col_start)[:, None], 0.0, solved)
        solved = solved.at[col_start:col_start + PW].set(factor)
        later_rows = solved[col_start + PW:W]
        update = jnp.dot(solved, later_rows.T, precision=lax.Precision.HIGHEST)
        trailing = front_rows[:, col_start + PW:] - jnp.where((global_row >= col_start + PW)[:, None], update, 0.0)
        front_rows = jnp.concatenate([front_rows[:, :col_start], solved, trailing], axis=1)
    front_rows = front_rows.at[:NPANEL * PW, NPANEL * PW:].set(0.0)
    return front_rows

def assemble(front_index, front_block, size_now, blocks, targets, places):
    row_count = CYCLE // BLK
    front_rows = front_block.reshape(FMAX, W)
    global_row = jnp.arange(FMAX, dtype=jnp.int32)
    front_rows = jnp.where((global_row < size_now)[:, None], front_rows, 0.0)

    def add_block(index, current):
        row_start = ((places[index] * row_count + index % row_count) * BLK).astype(jnp.int32)
        present = lax.dynamic_slice_in_dim(current, row_start, BLK, 0)
        arriving = jnp.where(targets[index] == front_index, blocks[index], 0.0)
        return lax.dynamic_update_slice_in_dim(current, present + arriving, row_start, 0)
    return lax.fori_loop(0, blocks.shape[0], add_block, front_rows)

def reference(front_matrix, front_sizes, contrib, dest_front, dest_local):
    row_count = CYCLE // BLK
    blocks = contrib.reshape(FRONTS * KB * row_count, BLK, W)
    targets = dest_front.reshape(-1)
    places = dest_local.reshape(-1)

    def one_front(front_index):
        assembled = assemble(front_index, front_matrix[front_index], front_sizes[front_index], blocks, targets, places)
        return factor_front(assembled).reshape(LOCB, CYCLE, W)
    return lax.map(one_front, jnp.arange(FRONTS, dtype=jnp.int32))
```

```python
import functools

import jax
import jax.numpy as jnp
from jax import lax
from jax.experimental import pallas as pl
from jax.experimental.pallas import tpu as pltpu
from jax.sharding import PartitionSpec as P

F = 8
R = 8
B = 128
LB = 12
HW = 1536
PC = 1024
NB = PC // B
KD = 256
MESH = pl.DeviceIdType.MESH
ANY = pl.BlockSpec(memory_space=pl.ANY)
VM = pl.BlockSpec(memory_space=pltpu.VMEM)
F32 = jnp.float32
MIB = 2**20


def split(x):
    hi = x.astype(jnp.bfloat16)
    return hi, (x - hi.astype(F32)).astype(jnp.bfloat16)


def left3(hi, lo):
    return jnp.concatenate([hi, lo, hi], 1)


def right3(hi, lo):
    return jnp.concatenate([hi, hi, lo], 1)


def dot_nt(a, b):
    return lax.dot_general(a, b, (((1,), (1,)), ((), ())), preferred_element_type=F32)


def dot_nn(a, b):
    return lax.dot_general(a, b, (((1,), (0,)), ((), ())), preferred_element_type=F32)


def dot3(a, b):
    return dot_nt(left3(*split(a)), right3(*split(b)))


def dot3_nn(a, b):
    bh, bl = split(b)
    return dot_nn(left3(*split(a)), jnp.concatenate([bh, bh, bl], 0))


def pack_kernel(which_ref, in_ref, out_ref):
    out_ref[...] = in_ref[...]


def pack(contrib, which):
    return pl.pallas_call(
        pack_kernel,
        grid_spec=pltpu.PrefetchScalarGridSpec(
            num_scalar_prefetch=1,
            grid=(F,),
            in_specs=[pl.BlockSpec((1, B, HW), lambda f, which: (which[f], 0, 0))],
            out_specs=pl.BlockSpec((1, B, HW), lambda f, which: (f, 0, 0)),
        ),
        out_shape=jax.ShapeDtypeStruct((F, B, HW), F32),
    )(which, contrib)


def first_exchange(front_ref, pack_ref, place_ref, piv_ref, inc_ref, got_ref, psend, precv, fsend, asend, arecv, lsend, lrecv, local):
    f = lax.axis_index("front")
    r = lax.axis_index("row")
    c = lax.axis_index("col")
    barrier = pltpu.get_barrier_semaphore()

    for d in range(1, F):
        pl.semaphore_signal(barrier, inc=1, device_id={"front": lax.rem(f + d, F)}, device_id_type=MESH)
    pl.semaphore_signal(barrier, inc=1, device_id={"col": 1 - c}, device_id_type=MESH)

    @pl.when(c == 0)
    def _():
        for d in range(1, R):
            pl.semaphore_signal(barrier, inc=1, device_id={"row": lax.rem(r + d, R)}, device_id_type=MESH)
        pl.semaphore_wait(barrier, F - 1 + 1 + R - 1)

    @pl.when(c == 1)
    def _():
        pl.semaphore_wait(barrier, F - 1 + 1)

    def pivot_copy(i, d):
        w = (i + 1) * B
        return pltpu.make_async_remote_copy(
            src_ref=front_ref.at[0, :, pl.ds(0, w)],
            dst_ref=piv_ref.at[i, :, pl.ds(0, w)],
            send_sem=psend.at[d],
            recv_sem=precv.at[i],
            device_id={"row": lax.rem(r + d, R)},
            device_id_type=MESH,
        )

    def pivot_own(i):
        w = (i + 1) * B
        return pltpu.make_async_copy(front_ref.at[0, :, pl.ds(0, w)], piv_ref.at[i, :, pl.ds(0, w)], local.at[0])

    def pivot_hand(i, own):
        w = (i + 1) * B
        return pltpu.make_async_remote_copy(
            src_ref=front_ref.at[0, :, pl.ds(0, w)] if own else piv_ref.at[i, :, pl.ds(0, w)],
            dst_ref=piv_ref.at[i, :, pl.ds(0, w)],
            send_sem=fsend.at[i],
            recv_sem=precv.at[i],
            device_id={"col": 1},
            device_id_type=MESH,
        )

    def contrib_copy(d):
        to = lax.rem(f + d, F)
        return pltpu.make_async_remote_copy(
            src_ref=pack_ref.at[to, :, pl.ds(0, PC)],
            dst_ref=inc_ref.at[f, :, pl.ds(0, PC)],
            send_sem=asend.at[d],
            recv_sem=arecv.at[d],
            device_id={"front": to},
            device_id_type=MESH,
        )

    def place_copy(d):
        to = lax.rem(f + d, F)
        return pltpu.make_async_remote_copy(
            src_ref=place_ref.at[to],
            dst_ref=got_ref.at[f],
            send_sem=lsend.at[d],
            recv_sem=lrecv.at[d],
            device_id={"front": to},
            device_id_type=MESH,
        )

    @pl.when(c == 0)
    def _():
        for i in range(R):
            @pl.when(r == i)
            def _():
                for d in range(1, R):
                    pivot_copy(i, d).start()
                pivot_hand(i, True).start()
                pivot_own(i).start()
        for d in range(1, F):
            contrib_copy(d).start()

    for d in range(1, F):
        place_copy(d).start()
    own_inc = pltpu.make_async_copy(pack_ref.at[f], inc_ref.at[f], local.at[1])
    own_inc.start()
    own_place = pltpu.make_async_copy(place_ref.at[f], got_ref.at[f], local.at[2])
    own_place.start()

    @pl.when(c == 0)
    def _():
        for i in range(R):
            @pl.when(r != i)
            def _():
                pivot_hand(i, False).wait_recv()
                pivot_hand(i, False).start()
        for i in range(R):
            @pl.when(r == i)
            def _():
                for d in range(1, R):
                    pivot_copy(i, d).wait_send()
                pivot_own(i).wait()
            pivot_hand(i, False).wait_send()
        for d in range(1, F):
            contrib_copy(d).wait()

    @pl.when(c == 1)
    def _():
        for i in range(R):
            pivot_hand(i, False).wait_recv()

    for d in range(1, F):
        place_copy(d).wait()
    own_inc.wait()
    own_place.wait()


def exchange_one(front, packed, places):
    return pl.pallas_call(
        first_exchange,
        out_shape=(
            jax.ShapeDtypeStruct((R, B, PC), F32),
            jax.ShapeDtypeStruct((F, B, HW), F32),
            jax.ShapeDtypeStruct((F, 8, 128), jnp.int32),
        ),
        in_specs=[ANY] * 3,
        out_specs=(ANY,) * 3,
        scratch_shapes=[
            pltpu.SemaphoreType.DMA((R,)),
            pltpu.SemaphoreType.DMA((R,)),
            pltpu.SemaphoreType.DMA((R,)),
            pltpu.SemaphoreType.DMA((F,)),
            pltpu.SemaphoreType.DMA((F,)),
            pltpu.SemaphoreType.DMA((F,)),
            pltpu.SemaphoreType.DMA((F,)),
            pltpu.SemaphoreType.DMA((3,)),
        ],
        compiler_params=pltpu.CompilerParams(collective_id=0, has_side_effects=True),
    )(front, packed, places)


def second_exchange(panel_ref, pack_ref, own_ref, win_ref, inc_ref, ssend, srecv, wsend, wrecv, vsend, vrecv, asend, arecv, local):
    f = lax.axis_index("front")
    r = lax.axis_index("row")
    c = lax.axis_index("col")
    barrier = pltpu.get_barrier_semaphore()

    for d in range(1, F):
        pl.semaphore_signal(barrier, inc=1, device_id={"front": lax.rem(f + d, F)}, device_id_type=MESH)
    for d in range(R):
        pl.semaphore_signal(barrier, inc=1, device_id={"row": lax.rem(r + d, R), "col": 1 - c}, device_id_type=MESH)

    @pl.when(c == 0)
    def _():
        for d in range(1, R):
            pl.semaphore_signal(barrier, inc=1, device_id={"row": lax.rem(r + d, R)}, device_id_type=MESH)
        pl.semaphore_wait(barrier, F - 1 + R + R - 1)

    @pl.when(c == 1)
    def _():
        pl.semaphore_wait(barrier, F - 1 + R)

    hand = pltpu.make_async_remote_copy(
        src_ref=panel_ref, dst_ref=own_ref, send_sem=ssend, recv_sem=srecv, device_id={"col": 1}, device_id_type=MESH
    )

    def second_round(d):
        return pltpu.make_async_remote_copy(
            src_ref=panel_ref.at[1],
            dst_ref=win_ref.at[4 + r],
            send_sem=wsend.at[d],
            recv_sem=wrecv.at[d],
            device_id={"row": lax.rem(r + d, R), "col": 1},
            device_id_type=MESH,
        )

    def first_round_high(d):
        return pltpu.make_async_remote_copy(
            src_ref=panel_ref.at[0],
            dst_ref=win_ref.at[r - 4],
            send_sem=vsend.at[d],
            recv_sem=vrecv.at[r - 4],
            device_id={"row": lax.rem(r + d, R), "col": 1},
            device_id_type=MESH,
        )

    def first_round_low(d):
        return pltpu.make_async_remote_copy(
            src_ref=panel_ref.at[0],
            dst_ref=win_ref.at[r],
            send_sem=vsend.at[d],
            recv_sem=vrecv.at[r],
            device_id={"row": lax.rem(r + d, R)},
            device_id_type=MESH,
        )

    def landed(i):
        return pltpu.make_async_remote_copy(
            src_ref=panel_ref.at[0],
            dst_ref=win_ref.at[i],
            send_sem=vsend.at[0],
            recv_sem=vrecv.at[i],
            device_id={"col": 1 - c},
            device_id_type=MESH,
        )

    def contrib_low(d):
        to = lax.rem(f + d, F)
        return pltpu.make_async_remote_copy(
            src_ref=pack_ref.at[to, :, pl.ds(PC, HW - PC)],
            dst_ref=inc_ref.at[f, :, pl.ds(PC, HW - PC)],
            send_sem=asend.at[d],
            recv_sem=arecv.at[d],
            device_id={"front": to},
            device_id_type=MESH,
        )

    def contrib_high(d):
        to = lax.rem(f + d, F)
        return pltpu.make_async_remote_copy(
            src_ref=pack_ref.at[to],
            dst_ref=inc_ref.at[f],
            send_sem=asend.at[d],
            recv_sem=arecv.at[d],
            device_id={"front": to},
            device_id_type=MESH,
        )

    keep_win = pltpu.make_async_copy(panel_ref.at[0], win_ref.at[lax.rem(r, 4)], local.at[0])
    keep_own = pltpu.make_async_copy(panel_ref, own_ref, local.at[1])
    own_inc = pltpu.make_async_copy(pack_ref.at[f], inc_ref.at[f], local.at[2])

    @pl.when(c == 0)
    def _():
        for d in range(R):
            second_round(d).start()

        @pl.when(r >= 4)
        def _():
            for d in range(R):
                first_round_high(d).start()

        @pl.when(r < 4)
        def _():
            for d in range(1, R):
                first_round_low(d).start()
            keep_win.start()

        hand.start()
        for d in range(1, F):
            contrib_low(d).start()
        keep_own.start()

    @pl.when(c == 1)
    def _():
        for d in range(1, F):
            contrib_high(d).start()

    own_inc.start()

    @pl.when(c == 0)
    def _():
        for d in range(R):
            second_round(d).wait_send()

        @pl.when(r >= 4)
        def _():
            for d in range(R):
                first_round_high(d).wait_send()

        @pl.when(r < 4)
        def _():
            for d in range(1, R):
                first_round_low(d).wait_send()
            keep_win.wait()

        for i in range(4):
            @pl.when(r != i)
            def _():
                landed(i).wait_recv()

        hand.wait_send()
        for d in range(1, F):
            contrib_low(d).wait()
        keep_own.wait()

    @pl.when(c == 1)
    def _():
        hand.wait_recv()
        for d in range(R):
            second_round(d).wait_recv()
        for i in range(4):
            landed(i).wait_recv()
        for d in range(1, F):
            contrib_high(d).wait()

    own_inc.wait()


def exchange_two(panel, packed):
    return pl.pallas_call(
        second_exchange,
        out_shape=(
            jax.ShapeDtypeStruct((LB - 1, B, PC), F32),
            jax.ShapeDtypeStruct((12, B, PC), F32),
            jax.ShapeDtypeStruct((F, B, HW), F32),
        ),
        in_specs=[ANY] * 2,
        out_specs=(ANY,) * 3,
        scratch_shapes=[
            pltpu.SemaphoreType.DMA,
            pltpu.SemaphoreType.DMA,
            pltpu.SemaphoreType.DMA((R,)),
            pltpu.SemaphoreType.DMA((R,)),
            pltpu.SemaphoreType.DMA((R,)),
            pltpu.SemaphoreType.DMA((4,)),
            pltpu.SemaphoreType.DMA((F,)),
            pltpu.SemaphoreType.DMA((F,)),
            pltpu.SemaphoreType.DMA((3,)),
        ],
        compiler_params=pltpu.CompilerParams(collective_id=1, has_side_effects=True),
    )(panel, packed)


def assemble_kernel(meta_ref, front_ref, inc_ref, out_ref):
    lb = pl.program_id(0) + 1
    valid = (lb * R + meta_ref[0]) * B < meta_ref[2]
    out_ref[...] = jnp.where(valid, front_ref[...], 0.0)
    for s in range(F):
        @pl.when(meta_ref[3 + s] == lb)
        def _():
            out_ref[...] += inc_ref[s : s + 1]


def assemble(meta, front, inc):
    return pl.pallas_call(
        assemble_kernel,
        grid_spec=pltpu.PrefetchScalarGridSpec(
            num_scalar_prefetch=1,
            grid=(LB - 1,),
            in_specs=[
                pl.BlockSpec((1, B, PC), lambda i, meta: (i + 1, 0, 0)),
                pl.BlockSpec((F, B, PC), lambda i, meta: (0, 0, 0)),
            ],
            out_specs=pl.BlockSpec((1, B, PC), lambda i, meta: (i, 0, 0)),
        ),
        out_shape=jax.ShapeDtypeStruct((LB - 1, B, PC), F32),
        compiler_params=pltpu.CompilerParams(vmem_limit_bytes=32 * MIB),
    )(meta, front, inc)


def recip(x):
    first = pl.reciprocal(x, approx=True)
    return first * (2.0 - x * first)


def lane_spread(x, k):
    return jnp.broadcast_to(x[:, k : k + 1], (8, B))


def row_spread(x, j):
    return jnp.broadcast_to(x[j : j + 1, :], (8, B))


def factor_block(sym):
    sub = lax.broadcasted_iota(jnp.int32, (8, B), 0)
    lane = lax.broadcasted_iota(jnp.int32, (8, B), 1)
    count = B // 8
    rows = [sym[q * 8 : (q + 1) * 8, :] for q in range(count)]
    eyes = [jnp.where(lane == sub + q * 8, 1.0, 0.0).astype(F32) for q in range(count)]
    factor, inverse = [], []
    for p in range(count):
        v, e = rows[p], eyes[p]
        c = [lane_spread(v, p * 8 + k) for k in range(8)]
        more = p < count - 1
        if more:
            v2, e2 = rows[p + 1], eyes[p + 1]
            c2 = [lane_spread(v2, p * 8 + k) for k in range(8)]
        diagonal = None
        for j in range(8):
            pivot = row_spread(c[j], j)
            diagonal = pivot if diagonal is None else jnp.where(sub == j, pivot, diagonal)
            over = recip(pivot)
            rv, re = row_spread(v, j), row_spread(e, j)
            m = jnp.where(sub > j, c[j] * over, 0.0)
            if more:
                m2 = c2[j] * over
            for k in range(j + 1, 8):
                s = row_spread(c[k], j)
                c[k] = c[k] - m * s
                if more:
                    c2[k] = c2[k] - m2 * s
            v = v - m * rv
            e = e - m * re
            if more:
                v2 = v2 - m2 * rv
                e2 = e2 - m2 * re
        scale = lax.rsqrt(diagonal)
        factor.append(jnp.where(lane >= sub + p * 8, v * scale, 0.0))
        inverse.append(e * scale)
        if more:
            rows[p + 1], eyes[p + 1] = v2, e2
        if p < count - 2:
            t = (v * recip(diagonal)).T
            rv = [row_spread(v, j) for j in range(8)]
            re = [row_spread(e, j) for j in range(8)]
            for q in range(p + 2, count):
                tq = t[q * 8 : (q + 1) * 8, :]
                for j in range(8):
                    m = jnp.broadcast_to(tq[:, j : j + 1], (8, B))
                    rows[q] = rows[q] - m * rv[j]
                    eyes[q] = eyes[q] - m * re[j]
    return jnp.concatenate(factor, 0), jnp.concatenate(inverse, 0)


def cholesky_kernel(a_ref, l_ref, i_ref, x_ref):
    l_ref[...] = a_ref[...]
    row_id = lax.broadcasted_iota(jnp.int32, (B, B), 0)
    col_id = lax.broadcasted_iota(jnp.int32, (B, B), 1)

    def step(k, carry):
        o = pl.multiple_of(k * B, B)
        d = l_ref[pl.ds(o, B), pl.ds(o, B)]
        lt, li = factor_block(jnp.where(row_id >= col_id, d, d.T))
        l_ref[pl.ds(o, B), pl.ds(o, B)] = lt.T
        x_ref[k] = li

        def trailing(kk):
            def run():
                base = (kk + 1) * B
                x = dot3(l_ref[base:, kk * B : base], li)
                l_ref[base:, kk * B : base] = x
                xh, xl = split(x)
                xa, xb = left3(xh, xl), right3(xh, xl)
                for j in range(kk + 1, NB):
                    jo = (j - kk - 1) * B
                    l_ref[j * B :, j * B : (j + 1) * B] -= dot_nt(xa[jo:], xb[jo : jo + B])

            return run

        for kk in range(NB - 1):
            pl.when(k == kk)(trailing(kk))
        return carry

    lax.fori_loop(0, NB, step, 0)
    for i in range(NB - 1):
        l_ref[i * B : (i + 1) * B, (i + 1) * B :] = jnp.zeros((B, (NB - 1 - i) * B), F32)
    for i in range(NB // 2):
        low, high = x_ref[2 * i], x_ref[2 * i + 1]
        between = l_ref[(2 * i + 1) * B : (2 * i + 2) * B, 2 * i * B : (2 * i + 1) * B]
        i_ref[i, :B, :B] = low
        i_ref[i, :B, B:] = jnp.zeros((B, B), F32)
        i_ref[i, B:, :B] = -dot3_nn(high, dot3_nn(between, low))
        i_ref[i, B:, B:] = high


def cholesky(a):
    return pl.pallas_call(
        cholesky_kernel,
        out_shape=(
            jax.ShapeDtypeStruct((PC, PC), F32),
            jax.ShapeDtypeStruct((PC // KD, KD, KD), F32),
        ),
        in_specs=[VM],
        out_specs=(VM, VM),
        scratch_shapes=[pltpu.VMEM((NB, B, B), F32)],
        compiler_params=pltpu.CompilerParams(vmem_limit_bytes=48 * MIB),
    )(a)


def final_kernel(meta_ref, front_ref, inc_ref, panel_ref, win_ref, l_ref, i_ref, out_ref, ph, plo, wh, wl, l3):
    t = pl.program_id(0)
    col = meta_ref[1]
    steps = PC // KD

    def solve(blocks, source_ref, hi_ref, lo_ref, at):
        rows = blocks * B
        his, los = [], []
        for k in range(steps):
            cols = slice(k * KD, (k + 1) * KD)
            a = source_ref[pl.ds(at, blocks), :, cols].reshape(rows, KD)
            for m in range(k):
                a = a - dot_nt(
                    left3(his[m], los[m]), l3[cols, 3 * m * KD : 3 * (m + 1) * KD]
                )
            p = dot3(a, i_ref[k])
            hi, lo = split(p)
            his.append(hi)
            los.append(lo)
            hi_ref[pl.ds(at * B, rows), cols] = hi
            lo_ref[pl.ds(at * B, rows), cols] = lo

    @pl.when(t == 0)
    def _():
        for m in range(steps - 1):
            hi, lo = split(l_ref[:, m * KD : (m + 1) * KD])
            l3[:, 3 * m * KD : 3 * (m + 1) * KD] = right3(hi, lo)
        solve(6, panel_ref, ph, plo, 0)
        solve(5, panel_ref, ph, plo, 6)
        solve(4, win_ref, wh, wl, 0)

        @pl.when(col == 1)
        def _():
            solve(4, win_ref, wh, wl, 4)
            solve(4, win_ref, wh, wl, 8)

    @pl.when((col == 0) & (t < steps))
    def _():
        row = pl.multiple_of(meta_ref[0] * B, B)
        for k in range(steps):
            @pl.when(t == k)
            def _():
                cols = slice(k * KD, (k + 1) * KD)
                out_ref[0] = l_ref[pl.ds(row, B), cols]
                out_ref[1:] = (ph[:, cols].astype(F32) + plo[:, cols].astype(F32)).reshape(LB - 1, B, KD)

    @pl.when((col == 1) | (t >= steps))
    def _():
        start = pl.multiple_of((t - jnp.where(col == 0, steps, 0)) * KD, KD)
        w_hi, w_lo = wh[pl.ds(start, KD), :], wl[pl.ds(start, KD), :]
        update = dot_nt(ph[...], w_hi) + dot_nt(plo[...], w_hi) + dot_nt(ph[...], w_lo)
        out_ref[0] = jnp.zeros((B, KD), F32)
        for lb in range(1, LB):
            valid = (lb * R + meta_ref[0]) * B < meta_ref[2]
            out_ref[lb] = jnp.where(valid, front_ref[lb], 0.0) - update[(lb - 1) * B : lb * B]
        for s in range(F):
            place = meta_ref[3 + s]

            @pl.when(place >= 0)
            def _():
                out_ref[pl.ds(place, 1)] += inc_ref[s : s + 1]


def final(meta, front, inc, panel, win, low, inv):
    tiles = HW // KD
    whole = dict(pipeline_mode=pl.Buffered(1))
    return pl.pallas_call(
        final_kernel,
        grid_spec=pltpu.PrefetchScalarGridSpec(
            num_scalar_prefetch=1,
            grid=(tiles,),
            in_specs=[
                pl.BlockSpec((LB, B, KD), lambda t, meta: (0, 0, t)),
                pl.BlockSpec((F, B, KD), lambda t, meta: (0, 0, t)),
                pl.BlockSpec((LB - 1, B, PC), lambda t, meta: (0, 0, 0), **whole),
                pl.BlockSpec((12, B, PC), lambda t, meta: (0, 0, 0), **whole),
                pl.BlockSpec((PC, PC), lambda t, meta: (0, 0), **whole),
                pl.BlockSpec((PC // KD, KD, KD), lambda t, meta: (0, 0, 0), **whole),
            ],
            out_specs=pl.BlockSpec((LB, B, KD), lambda t, meta: (0, 0, t)),
            scratch_shapes=[
                pltpu.VMEM(((LB - 1) * B, PC), jnp.bfloat16),
                pltpu.VMEM(((LB - 1) * B, PC), jnp.bfloat16),
                pltpu.VMEM((12 * B, PC), jnp.bfloat16),
                pltpu.VMEM((12 * B, PC), jnp.bfloat16),
                pltpu.VMEM((PC, 3 * (PC - KD)), jnp.bfloat16),
            ],
        ),
        out_shape=jax.ShapeDtypeStruct((LB, B, HW), F32),
        compiler_params=pltpu.CompilerParams(vmem_limit_bytes=60 * MIB),
    )(meta, front, inc, panel, win, low, inv)


def on_device(front_matrix, front_sizes, contrib, dest_front, dest_local):
    front = front_matrix[0]
    targets = dest_front[0, :, 0]
    places = dest_local[0, :, 0]
    select = targets[None, :] == jnp.arange(F, dtype=jnp.int32)[:, None]
    which = jnp.sum(jnp.where(select, jnp.arange(4, dtype=jnp.int32)[None, :], 0), axis=1)
    slot_place = jnp.where(jnp.any(select, axis=1), jnp.sum(jnp.where(select, places[None, :], 0), axis=1), -1)
    packed = pack(contrib[0], which)
    sent_places = jnp.broadcast_to(slot_place[:, None, None], (F, 8, 128))
    pivot, inc, got = exchange_one(front, packed, sent_places)
    row_col = jnp.stack([lax.axis_index("row"), lax.axis_index("col"), front_sizes[0]]).astype(jnp.int32)
    meta = jnp.concatenate([row_col, got[:, 0, 0]])
    panel = assemble(meta, front, inc)
    own, win, inc_rest = exchange_two(panel, packed)
    low, inv = cholesky(pivot.reshape(PC, PC))
    out = final(meta, front, inc_rest, own, win, low, inv)
    return out[None]


def solution(mesh):
    return jax.shard_map(
        on_device,
        mesh=mesh,
        in_specs=(
            P("front", None, "row", "col"),
            P("front"),
            P("front", None, "row", "col"),
            P("front", None, "row"),
            P("front", None, "row"),
        ),
        out_specs=P("front", None, "row", "col"),
        check_vma=False,
    )
```

```python
import functools

import jax
import jax.numpy as jnp
from jax import lax
from jax.experimental import pallas as pl
from jax.experimental.pallas import tpu as pltpu
from jax.sharding import PartitionSpec as P

F = 8
R = 8
B = 128
LB = 12
HW = 1536
PC = 1024
NB = PC // B
KD = 256
MESH = pl.DeviceIdType.MESH
ANY = pl.BlockSpec(memory_space=pl.ANY)
VM = pl.BlockSpec(memory_space=pltpu.VMEM)
F32 = jnp.float32
MIB = 2**20


def split(x):
    hi = x.astype(jnp.bfloat16)
    return hi, (x - hi.astype(F32)).astype(jnp.bfloat16)


def left3(hi, lo):
    return jnp.concatenate([hi, lo, hi], 1)


def right3(hi, lo):
    return jnp.concatenate([hi, hi, lo], 1)


def dot_nt(a, b):
    return lax.dot_general(a, b, (((1,), (1,)), ((), ())), preferred_element_type=F32)


def dot_nn(a, b):
    return lax.dot_general(a, b, (((1,), (0,)), ((), ())), preferred_element_type=F32)


def dot3(a, b):
    return dot_nt(left3(*split(a)), right3(*split(b)))


def dot3_nn(a, b):
    bh, bl = split(b)
    return dot_nn(left3(*split(a)), jnp.concatenate([bh, bh, bl], 0))


def pack_kernel(which_ref, in_ref, out_ref):
    out_ref[...] = in_ref[...]


def pack(contrib, which):
    return pl.pallas_call(
        pack_kernel,
        grid_spec=pltpu.PrefetchScalarGridSpec(
            num_scalar_prefetch=1,
            grid=(F,),
            in_specs=[pl.BlockSpec((1, B, HW), lambda f, which: (which[f], 0, 0))],
            out_specs=pl.BlockSpec((1, B, HW), lambda f, which: (f, 0, 0)),
        ),
        out_shape=jax.ShapeDtypeStruct((F, B, HW), F32),
    )(which, contrib)


def first_exchange(front_ref, pack_ref, place_ref, piv_ref, inc_ref, got_ref, psend, precv, fsend, asend, arecv, lsend, lrecv, local):
    f = lax.axis_index("front")
    r = lax.axis_index("row")
    c = lax.axis_index("col")
    barrier = pltpu.get_barrier_semaphore()

    for d in range(1, F):
        pl.semaphore_signal(barrier, inc=1, device_id={"front": lax.rem(f + d, F)}, device_id_type=MESH)
    pl.semaphore_signal(barrier, inc=1, device_id={"col": 1 - c}, device_id_type=MESH)

    @pl.when(c == 0)
    def _():
        for d in range(1, R):
            pl.semaphore_signal(barrier, inc=1, device_id={"row": lax.rem(r + d, R)}, device_id_type=MESH)
        pl.semaphore_wait(barrier, F - 1 + 1 + R - 1)

    @pl.when(c == 1)
    def _():
        pl.semaphore_wait(barrier, F - 1 + 1)

    def pivot_copy(i, d):
        w = (i + 1) * B
        return pltpu.make_async_remote_copy(
            src_ref=front_ref.at[0, :, pl.ds(0, w)],
            dst_ref=piv_ref.at[i, :, pl.ds(0, w)],
            send_sem=psend.at[d],
            recv_sem=precv.at[i],
            device_id={"row": lax.rem(r + d, R)},
            device_id_type=MESH,
        )

    def pivot_own(i):
        w = (i + 1) * B
        return pltpu.make_async_copy(front_ref.at[0, :, pl.ds(0, w)], piv_ref.at[i, :, pl.ds(0, w)], local.at[0])

    def pivot_hand(i, own):
        w = (i + 1) * B
        return pltpu.make_async_remote_copy(
            src_ref=front_ref.at[0, :, pl.ds(0, w)] if own else piv_ref.at[i, :, pl.ds(0, w)],
            dst_ref=piv_ref.at[i, :, pl.ds(0, w)],
            send_sem=fsend.at[i],
            recv_sem=precv.at[i],
            device_id={"col": 1},
            device_id_type=MESH,
        )

    def contrib_copy(d):
        to = lax.rem(f + d, F)
        return pltpu.make_async_remote_copy(
            src_ref=pack_ref.at[to, :, pl.ds(0, PC)],
            dst_ref=inc_ref.at[f, :, pl.ds(0, PC)],
            send_sem=asend.at[d],
            recv_sem=arecv.at[d],
            device_id={"front": to},
            device_id_type=MESH,
        )

    def place_copy(d):
        to = lax.rem(f + d, F)
        return pltpu.make_async_remote_copy(
            src_ref=place_ref.at[to],
            dst_ref=got_ref.at[f],
            send_sem=lsend.at[d],
            recv_sem=lrecv.at[d],
            device_id={"front": to},
            device_id_type=MESH,
        )

    @pl.when(c == 0)
    def _():
        for i in range(R):
            @pl.when(r == i)
            def _():
                for d in range(1, R):
                    pivot_copy(i, d).start()
                pivot_hand(i, True).start()
                pivot_own(i).start()
        for d in range(1, F):
            contrib_copy(d).start()

    for d in range(1, F):
        place_copy(d).start()
    own_inc = pltpu.make_async_copy(pack_ref.at[f], inc_ref.at[f], local.at[1])
    own_inc.start()
    own_place = pltpu.make_async_copy(place_ref.at[f], got_ref.at[f], local.at[2])
    own_place.start()

    @pl.when(c == 0)
    def _():
        for i in range(R):
            @pl.when(r != i)
            def _():
                pivot_hand(i, False).wait_recv()
                pivot_hand(i, False).start()
        for i in range(R):
            @pl.when(r == i)
            def _():
                for d in range(1, R):
                    pivot_copy(i, d).wait_send()
                pivot_own(i).wait()
            pivot_hand(i, False).wait_send()
        for d in range(1, F):
            contrib_copy(d).wait()

    @pl.when(c == 1)
    def _():
        for i in range(R):
            pivot_hand(i, False).wait_recv()

    for d in range(1, F):
        place_copy(d).wait()
    own_inc.wait()
    own_place.wait()


def exchange_one(front, packed, places):
    return pl.pallas_call(
        first_exchange,
        out_shape=(
            jax.ShapeDtypeStruct((R, B, PC), F32),
            jax.ShapeDtypeStruct((F, B, HW), F32),
            jax.ShapeDtypeStruct((F, 8, 128), jnp.int32),
        ),
        in_specs=[ANY] * 3,
        out_specs=(ANY,) * 3,
        scratch_shapes=[
            pltpu.SemaphoreType.DMA((R,)),
            pltpu.SemaphoreType.DMA((R,)),
            pltpu.SemaphoreType.DMA((R,)),
            pltpu.SemaphoreType.DMA((F,)),
            pltpu.SemaphoreType.DMA((F,)),
            pltpu.SemaphoreType.DMA((F,)),
            pltpu.SemaphoreType.DMA((F,)),
            pltpu.SemaphoreType.DMA((3,)),
        ],
        compiler_params=pltpu.CompilerParams(collective_id=0, has_side_effects=True),
    )(front, packed, places)


def second_exchange(panel_ref, pack_ref, a_ref, own_ref, win_ref, inc_ref, l_ref, i_ref, x_ref, ssend, srecv, wsend, wrecv, vsend, vrecv, asend, arecv, local):
    f = lax.axis_index("front")
    r = lax.axis_index("row")
    c = lax.axis_index("col")
    barrier = pltpu.get_barrier_semaphore()

    for d in range(1, F):
        pl.semaphore_signal(barrier, inc=1, device_id={"front": lax.rem(f + d, F)}, device_id_type=MESH)
    for d in range(R):
        pl.semaphore_signal(barrier, inc=1, device_id={"row": lax.rem(r + d, R), "col": 1 - c}, device_id_type=MESH)

    @pl.when(c == 0)
    def _():
        for d in range(1, R):
            pl.semaphore_signal(barrier, inc=1, device_id={"row": lax.rem(r + d, R)}, device_id_type=MESH)
        pl.semaphore_wait(barrier, F - 1 + R + R - 1)

    @pl.when(c == 1)
    def _():
        pl.semaphore_wait(barrier, F - 1 + R)

    hand = pltpu.make_async_remote_copy(
        src_ref=panel_ref, dst_ref=own_ref, send_sem=ssend, recv_sem=srecv, device_id={"col": 1}, device_id_type=MESH
    )

    def second_round(d):
        return pltpu.make_async_remote_copy(
            src_ref=panel_ref.at[1],
            dst_ref=win_ref.at[4 + r],
            send_sem=wsend.at[d],
            recv_sem=wrecv.at[d],
            device_id={"row": lax.rem(r + d, R), "col": 1},
            device_id_type=MESH,
        )

    def first_round_high(d):
        return pltpu.make_async_remote_copy(
            src_ref=panel_ref.at[0],
            dst_ref=win_ref.at[r - 4],
            send_sem=vsend.at[d],
            recv_sem=vrecv.at[r - 4],
            device_id={"row": lax.rem(r + d, R), "col": 1},
            device_id_type=MESH,
        )

    def first_round_low(d):
        return pltpu.make_async_remote_copy(
            src_ref=panel_ref.at[0],
            dst_ref=win_ref.at[r],
            send_sem=vsend.at[d],
            recv_sem=vrecv.at[r],
            device_id={"row": lax.rem(r + d, R)},
            device_id_type=MESH,
        )

    def landed(i):
        return pltpu.make_async_remote_copy(
            src_ref=panel_ref.at[0],
            dst_ref=win_ref.at[i],
            send_sem=vsend.at[0],
            recv_sem=vrecv.at[i],
            device_id={"col": 1 - c},
            device_id_type=MESH,
        )

    def contrib_low(d):
        to = lax.rem(f + d, F)
        return pltpu.make_async_remote_copy(
            src_ref=pack_ref.at[to, :, pl.ds(PC, HW - PC)],
            dst_ref=inc_ref.at[f, :, pl.ds(PC, HW - PC)],
            send_sem=asend.at[d],
            recv_sem=arecv.at[d],
            device_id={"front": to},
            device_id_type=MESH,
        )

    def contrib_high(d):
        to = lax.rem(f + d, F)
        return pltpu.make_async_remote_copy(
            src_ref=pack_ref.at[to],
            dst_ref=inc_ref.at[f],
            send_sem=asend.at[d],
            recv_sem=arecv.at[d],
            device_id={"front": to},
            device_id_type=MESH,
        )

    keep_win = pltpu.make_async_copy(panel_ref.at[0], win_ref.at[lax.rem(r, 4)], local.at[0])
    own_inc = pltpu.make_async_copy(pack_ref.at[f], inc_ref.at[f], local.at[2])

    @pl.when(c == 0)
    def _():
        for d in range(R):
            second_round(d).start()

        @pl.when(r >= 4)
        def _():
            for d in range(R):
                first_round_high(d).start()

        @pl.when(r < 4)
        def _():
            for d in range(1, R):
                first_round_low(d).start()
            keep_win.start()

        hand.start()
        for d in range(1, F):
            contrib_low(d).start()

    @pl.when(c == 1)
    def _():
        for d in range(1, F):
            contrib_high(d).start()

    own_inc.start()

    cholesky_body(a_ref, l_ref, i_ref, x_ref)

    @pl.when(c == 0)
    def _():
        for d in range(R):
            second_round(d).wait_send()

        @pl.when(r >= 4)
        def _():
            for d in range(R):
                first_round_high(d).wait_send()

        @pl.when(r < 4)
        def _():
            for d in range(1, R):
                first_round_low(d).wait_send()
            keep_win.wait()

        for i in range(4):
            @pl.when(r != i)
            def _():
                landed(i).wait_recv()

        hand.wait_send()
        for d in range(1, F):
            contrib_low(d).wait()

    @pl.when(c == 1)
    def _():
        hand.wait_recv()
        for d in range(R):
            second_round(d).wait_recv()
        for i in range(4):
            landed(i).wait_recv()
        for d in range(1, F):
            contrib_high(d).wait()

    own_inc.wait()


def exchange_two(panel, packed, pivot):
    return pl.pallas_call(
        second_exchange,
        out_shape=(
            jax.ShapeDtypeStruct((LB - 1, B, PC), F32),
            jax.ShapeDtypeStruct((12, B, PC), F32),
            jax.ShapeDtypeStruct((F, B, HW), F32),
            jax.ShapeDtypeStruct((PC, PC), F32),
            jax.ShapeDtypeStruct((PC // KD, KD, KD), F32),
        ),
        in_specs=[ANY, ANY, VM],
        out_specs=(ANY, ANY, ANY, VM, VM),
        scratch_shapes=[
            pltpu.VMEM((NB, B, B), F32),
            pltpu.SemaphoreType.DMA,
            pltpu.SemaphoreType.DMA,
            pltpu.SemaphoreType.DMA((R,)),
            pltpu.SemaphoreType.DMA((R,)),
            pltpu.SemaphoreType.DMA((R,)),
            pltpu.SemaphoreType.DMA((4,)),
            pltpu.SemaphoreType.DMA((F,)),
            pltpu.SemaphoreType.DMA((F,)),
            pltpu.SemaphoreType.DMA((3,)),
        ],
        compiler_params=pltpu.CompilerParams(collective_id=1, has_side_effects=True, vmem_limit_bytes=48 * MIB),
    )(panel, packed, pivot)


def assemble_kernel(meta_ref, front_ref, inc_ref, out_ref):
    lb = pl.program_id(0) + 1
    valid = (lb * R + meta_ref[0]) * B < meta_ref[2]
    out_ref[...] = jnp.where(valid, front_ref[...], 0.0)
    for s in range(F):
        @pl.when(meta_ref[3 + s] == lb)
        def _():
            out_ref[...] += inc_ref[s : s + 1]


def assemble(meta, front, inc):
    return pl.pallas_call(
        assemble_kernel,
        grid_spec=pltpu.PrefetchScalarGridSpec(
            num_scalar_prefetch=1,
            grid=(LB - 1,),
            in_specs=[
                pl.BlockSpec((1, B, PC), lambda i, meta: (i + 1, 0, 0)),
                pl.BlockSpec((F, B, PC), lambda i, meta: (0, 0, 0)),
            ],
            out_specs=pl.BlockSpec((1, B, PC), lambda i, meta: (i, 0, 0)),
        ),
        out_shape=jax.ShapeDtypeStruct((LB - 1, B, PC), F32),
        compiler_params=pltpu.CompilerParams(vmem_limit_bytes=32 * MIB),
    )(meta, front, inc)


def recip(x):
    first = pl.reciprocal(x, approx=True)
    return first * (2.0 - x * first)


def lane_spread(x, k):
    return jnp.broadcast_to(x[:, k : k + 1], (8, B))


def row_spread(x, j):
    return jnp.broadcast_to(x[j : j + 1, :], (8, B))


def factor_block(sym):
    sub = lax.broadcasted_iota(jnp.int32, (8, B), 0)
    lane = lax.broadcasted_iota(jnp.int32, (8, B), 1)
    count = B // 8
    rows = [sym[q * 8 : (q + 1) * 8, :] for q in range(count)]
    eyes = [jnp.where(lane == sub + q * 8, 1.0, 0.0).astype(F32) for q in range(count)]
    factor, inverse = [], []
    for p in range(count):
        v, e = rows[p], eyes[p]
        c = [lane_spread(v, p * 8 + k) for k in range(8)]
        more = p < count - 1
        if more:
            v2, e2 = rows[p + 1], eyes[p + 1]
            c2 = [lane_spread(v2, p * 8 + k) for k in range(8)]
        diagonal = None
        for j in range(8):
            pivot = row_spread(c[j], j)
            diagonal = pivot if diagonal is None else jnp.where(sub == j, pivot, diagonal)
            over = recip(pivot)
            rv, re = row_spread(v, j), row_spread(e, j)
            m = jnp.where(sub > j, c[j] * over, 0.0)
            if more:
                m2 = c2[j] * over
            for k in range(j + 1, 8):
                s = row_spread(c[k], j)
                c[k] = c[k] - m * s
                if more:
                    c2[k] = c2[k] - m2 * s
            v = v - m * rv
            e = e - m * re
            if more:
                v2 = v2 - m2 * rv
                e2 = e2 - m2 * re
        scale = lax.rsqrt(diagonal)
        factor.append(jnp.where(lane >= sub + p * 8, v * scale, 0.0))
        inverse.append(e * scale)
        if more:
            rows[p + 1], eyes[p + 1] = v2, e2
        if p < count - 2:
            t = (v * recip(diagonal)).T
            rv = [row_spread(v, j) for j in range(8)]
            re = [row_spread(e, j) for j in range(8)]
            for q in range(p + 2, count):
                tq = t[q * 8 : (q + 1) * 8, :]
                for j in range(8):
                    m = jnp.broadcast_to(tq[:, j : j + 1], (8, B))
                    rows[q] = rows[q] - m * rv[j]
                    eyes[q] = eyes[q] - m * re[j]
    return jnp.concatenate(factor, 0), jnp.concatenate(inverse, 0)


def cholesky_body(a_ref, l_ref, i_ref, x_ref):
    l_ref[...] = a_ref[...]
    row_id = lax.broadcasted_iota(jnp.int32, (B, B), 0)
    col_id = lax.broadcasted_iota(jnp.int32, (B, B), 1)

    def step(k, carry):
        o = pl.multiple_of(k * B, B)
        d = l_ref[pl.ds(o, B), pl.ds(o, B)]
        lt, li = factor_block(jnp.where(row_id >= col_id, d, d.T))
        l_ref[pl.ds(o, B), pl.ds(o, B)] = lt.T
        x_ref[k] = li

        def trailing(kk):
            def run():
                base = (kk + 1) * B
                x = dot3(l_ref[base:, kk * B : base], li)
                l_ref[base:, kk * B : base] = x
                xh, xl = split(x)
                xa, xb = left3(xh, xl), right3(xh, xl)
                for j in range(kk + 1, NB):
                    jo = (j - kk - 1) * B
                    l_ref[j * B :, j * B : (j + 1) * B] -= dot_nt(xa[jo:], xb[jo : jo + B])

            return run

        for kk in range(NB - 1):
            pl.when(k == kk)(trailing(kk))
        return carry

    lax.fori_loop(0, NB, step, 0)
    for i in range(NB - 1):
        l_ref[i * B : (i + 1) * B, (i + 1) * B :] = jnp.zeros((B, (NB - 1 - i) * B), F32)
    for i in range(NB // 2):
        low, high = x_ref[2 * i], x_ref[2 * i + 1]
        between = l_ref[(2 * i + 1) * B : (2 * i + 2) * B, 2 * i * B : (2 * i + 1) * B]
        i_ref[i, :B, :B] = low
        i_ref[i, :B, B:] = jnp.zeros((B, B), F32)
        i_ref[i, B:, :B] = -dot3_nn(high, dot3_nn(between, low))
        i_ref[i, B:, B:] = high


def final_kernel(meta_ref, front_ref, inc_ref, panel_any, own_any, win_ref, l_ref, i_ref, out_ref, panel_ref, ph, plo, wh, wl, l3, sem):
    t = pl.program_id(0)
    col = meta_ref[1]
    steps = PC // KD

    def solve(blocks, source_ref, hi_ref, lo_ref, at):
        rows = blocks * B
        his, los = [], []
        for k in range(steps):
            cols = slice(k * KD, (k + 1) * KD)
            a = source_ref[pl.ds(at, blocks), :, cols].reshape(rows, KD)
            for m in range(k):
                a = a - dot_nt(
                    left3(his[m], los[m]), l3[cols, 3 * m * KD : 3 * (m + 1) * KD]
                )
            p = dot3(a, i_ref[k])
            hi, lo = split(p)
            his.append(hi)
            los.append(lo)
            hi_ref[pl.ds(at * B, rows), cols] = hi
            lo_ref[pl.ds(at * B, rows), cols] = lo

    @pl.when(t == 0)
    def _():
        @pl.when(col == 0)
        def _():
            pltpu.make_async_copy(panel_any, panel_ref, sem).start()

        @pl.when(col == 1)
        def _():
            pltpu.make_async_copy(own_any, panel_ref, sem).start()

        for m in range(steps - 1):
            hi, lo = split(l_ref[:, m * KD : (m + 1) * KD])
            l3[:, 3 * m * KD : 3 * (m + 1) * KD] = right3(hi, lo)
        pltpu.make_async_copy(panel_any, panel_ref, sem).wait()
        solve(6, panel_ref, ph, plo, 0)
        solve(5, panel_ref, ph, plo, 6)
        solve(4, win_ref, wh, wl, 0)

        @pl.when(col == 1)
        def _():
            solve(4, win_ref, wh, wl, 4)
            solve(4, win_ref, wh, wl, 8)

    @pl.when((col == 0) & (t < steps))
    def _():
        row = pl.multiple_of(meta_ref[0] * B, B)
        for k in range(steps):
            @pl.when(t == k)
            def _():
                cols = slice(k * KD, (k + 1) * KD)
                out_ref[0] = l_ref[pl.ds(row, B), cols]
                out_ref[1:] = (ph[:, cols].astype(F32) + plo[:, cols].astype(F32)).reshape(LB - 1, B, KD)

    @pl.when((col == 1) | (t >= steps))
    def _():
        start = pl.multiple_of((t - jnp.where(col == 0, steps, 0)) * KD, KD)
        w_hi, w_lo = wh[pl.ds(start, KD), :], wl[pl.ds(start, KD), :]
        update = dot_nt(ph[...], w_hi) + dot_nt(plo[...], w_hi) + dot_nt(ph[...], w_lo)
        out_ref[0] = jnp.zeros((B, KD), F32)
        for lb in range(1, LB):
            valid = (lb * R + meta_ref[0]) * B < meta_ref[2]
            out_ref[lb] = jnp.where(valid, front_ref[lb], 0.0) - update[(lb - 1) * B : lb * B]
        for s in range(F):
            place = meta_ref[3 + s]

            @pl.when(place >= 0)
            def _():
                out_ref[pl.ds(place, 1)] += inc_ref[s : s + 1]


def final(meta, front, inc, panel, own, win, low, inv):
    tiles = HW // KD
    whole = dict(pipeline_mode=pl.Buffered(1))
    return pl.pallas_call(
        final_kernel,
        grid_spec=pltpu.PrefetchScalarGridSpec(
            num_scalar_prefetch=1,
            grid=(tiles,),
            in_specs=[
                pl.BlockSpec((LB, B, KD), lambda t, meta: (0, 0, t)),
                pl.BlockSpec((F, B, KD), lambda t, meta: (0, 0, t)),
                ANY,
                ANY,
                pl.BlockSpec((12, B, PC), lambda t, meta: (0, 0, 0), **whole),
                pl.BlockSpec((PC, PC), lambda t, meta: (0, 0), **whole),
                pl.BlockSpec((PC // KD, KD, KD), lambda t, meta: (0, 0, 0), **whole),
            ],
            out_specs=pl.BlockSpec((LB, B, KD), lambda t, meta: (0, 0, t)),
            scratch_shapes=[
                pltpu.VMEM((LB - 1, B, PC), F32),
                pltpu.VMEM(((LB - 1) * B, PC), jnp.bfloat16),
                pltpu.VMEM(((LB - 1) * B, PC), jnp.bfloat16),
                pltpu.VMEM((12 * B, PC), jnp.bfloat16),
                pltpu.VMEM((12 * B, PC), jnp.bfloat16),
                pltpu.VMEM((PC, 3 * (PC - KD)), jnp.bfloat16),
                pltpu.SemaphoreType.DMA,
            ],
        ),
        out_shape=jax.ShapeDtypeStruct((LB, B, HW), F32),
        compiler_params=pltpu.CompilerParams(vmem_limit_bytes=60 * MIB),
    )(meta, front, inc, panel, own, win, low, inv)


def on_device(front_matrix, front_sizes, contrib, dest_front, dest_local):
    front = front_matrix[0]
    targets = dest_front[0, :, 0]
    places = dest_local[0, :, 0]
    select = targets[None, :] == jnp.arange(F, dtype=jnp.int32)[:, None]
    which = jnp.sum(jnp.where(select, jnp.arange(4, dtype=jnp.int32)[None, :], 0), axis=1)
    slot_place = jnp.where(jnp.any(select, axis=1), jnp.sum(jnp.where(select, places[None, :], 0), axis=1), -1)
    packed = pack(contrib[0], which)
    sent_places = jnp.broadcast_to(slot_place[:, None, None], (F, 8, 128))
    pivot, inc, got = exchange_one(front, packed, sent_places)
    row_col = jnp.stack([lax.axis_index("row"), lax.axis_index("col"), front_sizes[0]]).astype(jnp.int32)
    meta = jnp.concatenate([row_col, got[:, 0, 0]])
    panel = assemble(meta, front, inc)
    own, win, inc_rest, low, inv = exchange_two(panel, packed, pivot.reshape(PC, PC))
    out = final(meta, front, inc_rest, panel, own, win, low, inv)
    return out[None]


def solution(mesh):
    return jax.shard_map(
        on_device,
        mesh=mesh,
        in_specs=(
            P("front", None, "row", "col"),
            P("front"),
            P("front", None, "row", "col"),
            P("front", None, "row"),
            P("front", None, "row"),
        ),
        out_specs=P("front", None, "row", "col"),
        check_vma=False,
    )
```

```python
import functools

import jax
import jax.numpy as jnp
from jax import lax
from jax.experimental import pallas as pl
from jax.experimental.pallas import tpu as pltpu
from jax.sharding import PartitionSpec as P

F = 8
R = 8
B = 128
LB = 12
HW = 1536
PC = 1024
NB = PC // B
KD = 256
MESH = pl.DeviceIdType.MESH
ANY = pl.BlockSpec(memory_space=pl.ANY)
VM = pl.BlockSpec(memory_space=pltpu.VMEM)
F32 = jnp.float32
MIB = 2**20


def split(x):
    hi = x.astype(jnp.bfloat16)
    return hi, (x - hi.astype(F32)).astype(jnp.bfloat16)


def left3(hi, lo):
    return jnp.concatenate([hi, lo, hi], 1)


def right3(hi, lo):
    return jnp.concatenate([hi, hi, lo], 1)


def dot_nt(a, b):
    return lax.dot_general(a, b, (((1,), (1,)), ((), ())), preferred_element_type=F32)


def dot_nn(a, b):
    return lax.dot_general(a, b, (((1,), (0,)), ((), ())), preferred_element_type=F32)


def dot3(a, b):
    return dot_nt(left3(*split(a)), right3(*split(b)))


def dot3_nn(a, b):
    bh, bl = split(b)
    return dot_nn(left3(*split(a)), jnp.concatenate([bh, bh, bl], 0))


def recip(x):
    first = pl.reciprocal(x, approx=True)
    return first * (2.0 - x * first)


def lane_spread(x, k):
    return jnp.broadcast_to(x[:, k : k + 1], (8, B))


def row_spread(x, j):
    return jnp.broadcast_to(x[j : j + 1, :], (8, B))


def factor_block(sym):
    sub = lax.broadcasted_iota(jnp.int32, (8, B), 0)
    lane = lax.broadcasted_iota(jnp.int32, (8, B), 1)
    count = B // 8
    rows = [sym[q * 8 : (q + 1) * 8, :] for q in range(count)]
    eyes = [jnp.where(lane == sub + q * 8, 1.0, 0.0).astype(F32) for q in range(count)]
    factor, inverse = [], []
    for p in range(count):
        v, e = rows[p], eyes[p]
        c = [lane_spread(v, p * 8 + k) for k in range(8)]
        more = p < count - 1
        if more:
            v2, e2 = rows[p + 1], eyes[p + 1]
            c2 = [lane_spread(v2, p * 8 + k) for k in range(8)]
        diagonal = None
        for j in range(8):
            pivot = row_spread(c[j], j)
            diagonal = pivot if diagonal is None else jnp.where(sub == j, pivot, diagonal)
            over = recip(pivot)
            rv, re = row_spread(v, j), row_spread(e, j)
            m = jnp.where(sub > j, c[j] * over, 0.0)
            if more:
                m2 = c2[j] * over
            for k in range(j + 1, 8):
                s = row_spread(c[k], j)
                c[k] = c[k] - m * s
                if more:
                    c2[k] = c2[k] - m2 * s
            v = v - m * rv
            e = e - m * re
            if more:
                v2 = v2 - m2 * rv
                e2 = e2 - m2 * re
        scale = lax.rsqrt(diagonal)
        factor.append(jnp.where(lane >= sub + p * 8, v * scale, 0.0))
        inverse.append(e * scale)
        if more:
            rows[p + 1], eyes[p + 1] = v2, e2
        if p < count - 2:
            t = (v * recip(diagonal)).T
            rv = [row_spread(v, j) for j in range(8)]
            re = [row_spread(e, j) for j in range(8)]
            for q in range(p + 2, count):
                tq = t[q * 8 : (q + 1) * 8, :]
                for j in range(8):
                    m = jnp.broadcast_to(tq[:, j : j + 1], (8, B))
                    rows[q] = rows[q] - m * rv[j]
                    eyes[q] = eyes[q] - m * re[j]
    return jnp.concatenate(factor, 0), jnp.concatenate(inverse, 0)


def cholesky_body(a_ref, l_ref, i_ref, x_ref, after):
    for i in range(NB):
        l_ref[i * B : (i + 1) * B, : (i + 1) * B] = a_ref[i, :, : (i + 1) * B]
    row_id = lax.broadcasted_iota(jnp.int32, (B, B), 0)
    col_id = lax.broadcasted_iota(jnp.int32, (B, B), 1)

    def step(k, carry):
        o = pl.multiple_of(k * B, B)
        d = l_ref[pl.ds(o, B), pl.ds(o, B)]
        lt, li = factor_block(jnp.where(row_id >= col_id, d, d.T))
        l_ref[pl.ds(o, B), pl.ds(o, B)] = lt.T
        x_ref[k] = li

        def trailing(kk):
            def run():
                base = (kk + 1) * B
                x = dot3(l_ref[base:, kk * B : base], li)
                l_ref[base:, kk * B : base] = x
                xh, xl = split(x)
                xa, xb = left3(xh, xl), right3(xh, xl)
                for j in range(kk + 1, NB):
                    jo = (j - kk - 1) * B
                    l_ref[j * B :, j * B : (j + 1) * B] -= dot_nt(xa[jo:], xb[jo : jo + B])

            return run

        for kk in range(NB - 1):
            pl.when(k == kk)(trailing(kk))
        after(k)
        return carry

    lax.fori_loop(0, NB, step, 0)
    for i in range(NB - 1):
        l_ref[i * B : (i + 1) * B, (i + 1) * B :] = jnp.zeros((B, (NB - 1 - i) * B), F32)
    for i in range(NB // 2):
        low, high = x_ref[2 * i], x_ref[2 * i + 1]
        between = l_ref[(2 * i + 1) * B : (2 * i + 2) * B, 2 * i * B : (2 * i + 1) * B]
        i_ref[i, :B, :B] = low
        i_ref[i, :B, B:] = jnp.zeros((B, B), F32)
        i_ref[i, B:, :B] = -dot3_nn(high, dot3_nn(between, low))
        i_ref[i, B:, B:] = high


def exchange_kernel(
    front_ref, contrib_ref, dest_ref, local_ref, size_ref,
    panel_ref, win_ref, inc_ref, got_ref, l_ref, i_ref,
    x_ref, cont, packed, pan, inc_p, piv, place_v,
    psend, precv, fsend, asend, arecv, bsend, brecv, lsend, lrecv, hsend, hrecv, wsend, wrecv, gsend, local,
):
    f = lax.axis_index("front")
    r = lax.axis_index("row")
    c = lax.axis_index("col")
    y = lax.rem(r, 4)
    side = r - y
    across = lax.rem(r + 4, R)
    rest = HW - PC

    load_contrib = pltpu.make_async_copy(contrib_ref, cont, local.at[0])
    load_contrib.start()
    load_panel = pltpu.make_async_copy(front_ref.at[pl.ds(1, LB - 1), :, pl.ds(0, PC)], pan, local.at[1])

    @pl.when(c == 0)
    def _():
        load_panel.start()

    barrier = pltpu.get_barrier_semaphore()
    for d in range(1, F):
        pl.semaphore_signal(barrier, inc=1, device_id={"front": lax.rem(f + d, F)}, device_id_type=MESH)
        pl.semaphore_signal(barrier, inc=1, device_id={"row": lax.rem(r + d, R)}, device_id_type=MESH)
    for d in range(R):
        pl.semaphore_signal(barrier, inc=1, device_id={"row": lax.rem(r + d, R), "col": 1 - c}, device_id_type=MESH)
    pl.semaphore_wait(barrier, F - 1 + R - 1 + R)

    def send(src, dst, send_sem, recv_sem, **device):
        return pltpu.make_async_remote_copy(
            src_ref=src, dst_ref=dst, send_sem=send_sem, recv_sem=recv_sem, device_id=device, device_id_type=MESH
        )

    def pivot_copy(i, d):
        cols = pl.ds(0, (i + 1) * B)
        return send(front_ref.at[0, :, cols], piv.at[i, :, cols], psend.at[d], precv.at[i], row=lax.rem(r + d, R))

    def pivot_own(i):
        cols = pl.ds(0, (i + 1) * B)
        return pltpu.make_async_copy(front_ref.at[0, :, cols], piv.at[i, :, cols], local.at[2])

    def pivot_hand(i, own):
        cols = pl.ds(0, (i + 1) * B)
        src = front_ref.at[0, :, cols] if own else piv.at[i, :, cols]
        return send(src, piv.at[i, :, cols], fsend.at[i], precv.at[i], col=1)

    @pl.when(c == 0)
    def _():
        for i in range(R):
            @pl.when(r == i)
            def _():
                for d in range(1, R):
                    pivot_copy(i, d).start()
                pivot_hand(i, True).start()
                pivot_own(i).start()

    def contrib_panel(d):
        to = lax.rem(f + d, F)
        return send(packed.at[to, :, pl.ds(0, PC)], inc_p.at[f], asend.at[d], arecv.at[d], front=to)

    def contrib_low(d):
        to = lax.rem(f + d, F)
        cols = pl.ds(PC, rest)
        return send(packed.at[to, :, cols], inc_ref.at[f, :, cols], bsend.at[d], brecv.at[d], front=to)

    def contrib_high(d):
        to = lax.rem(f + d, F)
        return send(packed.at[to], inc_ref.at[f], bsend.at[d], brecv.at[d], front=to)

    def place_copy(d):
        to = lax.rem(f + d, F)
        return send(place_v.at[to], got_ref.at[f], lsend.at[d], lrecv.at[d], front=to)

    def choice(to):
        which, place = 0, -1
        for k in range(4):
            mine = dest_ref[k] == to
            which = jnp.where(mine, k, which)
            place = jnp.where(mine, local_ref[k], place)
        return which, place

    load_contrib.wait()

    @pl.when(c == 0)
    def _():
        def one(d, carry):
            to = lax.rem(f + d, F)
            which, _ = choice(to)
            packed[to, :, :PC] = cont[which, :, :PC]
            contrib_panel(d).start()
            return carry

        lax.fori_loop(1, F, one, 0)
        which, _ = choice(f)
        inc_p[f] = cont[which, :, :PC]

    def place_one(d, carry):
        to = lax.rem(f + d, F)
        _, place = choice(to)
        place_v[to] = jnp.full((8, B), place, jnp.int32)
        place_copy(d).start()
        return carry

    lax.fori_loop(1, F, place_one, 0)
    _, own_place = choice(f)
    got_ref[f] = jnp.full((8, B), own_place, jnp.int32)

    def pack_low(d, carry):
        to = lax.rem(f + d, F)
        which, _ = choice(to)
        packed[to, :, PC:] = cont[which, :, PC:]
        return carry

    def pack_high(d, carry):
        to = lax.rem(f + d, F)
        which, _ = choice(to)
        packed[to] = cont[which]
        return carry

    @pl.when(c == 0)
    def _():
        lax.fori_loop(0, F, pack_low, 0)

    @pl.when(c == 1)
    def _():
        lax.fori_loop(0, F, pack_high, 0)

    inc_own_low = pltpu.make_async_copy(packed.at[f, :, pl.ds(PC, rest)], inc_ref.at[f, :, pl.ds(PC, rest)], local.at[3])
    inc_own_high = pltpu.make_async_copy(packed.at[f], inc_ref.at[f], local.at[3])

    for d in range(1, F):
        place_copy(d).wait()

    @pl.when(c == 0)
    def _():
        for d in range(R):
            for i in range(R):
                @pl.when(lax.rem(r + d, R) == i)
                def _():
                    if d > 0:
                        pivot_hand(i, False).wait_recv()
                        pivot_hand(i, False).start()
                    else:
                        pivot_own(i).wait()

    @pl.when(c == 1)
    def _():
        for i in range(R):
            pivot_hand(i, False).wait_recv()

    near = (1, 3, 2)

    def row_at(d):
        return side + lax.rem(y + d, 4)

    def own_second(n):
        src, dst = pan.at[1], win_ref.at[4 + r]
        if n == 0:
            return send(src, dst, wsend.at[0], wrecv.at[4 + r], row=across, col=1)
        if n == 1:
            return send(src, dst, wsend.at[1], wrecv.at[4 + r], col=1)
        return send(src, dst, wsend.at[n], wrecv.at[4 + r], row=row_at(near[n - 2]), col=1)

    def own_high(n):
        src, dst, rs = pan.at[0], win_ref.at[r - 4], wrecv.at[r - 4]
        if n == 0:
            return send(src, dst, wsend.at[5], rs, row=across, col=1)
        if n == 1:
            return send(src, dst, wsend.at[6], rs, col=1)
        return send(src, dst, wsend.at[5 + n], rs, row=row_at(near[n - 2]), col=1)

    def own_low(n):
        src, dst, rs = pan.at[0], win_ref.at[r], wrecv.at[r]
        if n == 0:
            return send(src, dst, wsend.at[5], rs, row=across)
        return send(src, dst, wsend.at[6 + n], rs, row=row_at(near[n - 1]))

    keep_low = pltpu.make_async_copy(pan.at[0], win_ref.at[y], local.at[4])
    keep_panel = pltpu.make_async_copy(pan, panel_ref, local.at[5])
    hand = send(pan, panel_ref, hsend, hrecv, col=1)

    def landed(i):
        return send(pan.at[0], win_ref.at[i], gsend.at[0], wrecv.at[i], col=1 - c)

    def pass_second(n):
        at = 4 + across
        return send(win_ref.at[at], win_ref.at[at], gsend.at[n], wrecv.at[at], row=row_at(near[n]))

    def pass_first(n):
        return send(win_ref.at[y], win_ref.at[y], gsend.at[3 + n], wrecv.at[y], row=row_at(near[n]))

    def assemble(lb):
        valid = (lb * R + r) * B < size_ref[0]

        def eight(i, carry):
            at = pl.ds(pl.multiple_of(i * 8, 8), 8)
            total = jnp.where(valid, pan[lb - 1, at, :], 0.0)
            for s in range(F):
                mask = jnp.concatenate([got_ref[s]] * (PC // B), 1) == lb
                total = total + jnp.where(mask, inc_p[s, at, :], 0.0)
            pan[lb - 1, at, :] = total
            return carry

        lax.fori_loop(0, B // 8, eight, 0)

    def after(k):
        @pl.when((k == 1) & (c == 0))
        def _():
            load_panel.wait()
            for d in range(1, F):
                contrib_panel(d).wait()
            assemble(2)
            for n in range(5):
                own_second(n).start()
            assemble(1)

            @pl.when(r >= 4)
            def _():
                for n in range(5):
                    own_high(n).start()

            @pl.when(r < 4)
            def _():
                for n in range(4):
                    own_low(n).start()
                keep_low.start()

            for d in range(1, F):
                contrib_low(d).start()
            inc_own_low.start()

            def others(lb, carry):
                assemble(lb)
                return carry

            lax.fori_loop(3, LB, others, 0)
            hand.start()
            keep_panel.start()

        @pl.when((k == 1) & (c == 1))
        def _():
            for d in range(1, F):
                contrib_high(d).start()
            inc_own_high.start()

        @pl.when((k == 3) & (c == 0) & (r >= 4))
        def _():
            landed(y).wait_recv()
            for n in range(3):
                pass_first(n).start()

        @pl.when((k == 3) & (c == 1))
        def _():
            landed(4 + across).wait_recv()
            for n in range(3):
                pass_second(n).start()

            @pl.when(r < 4)
            def _():
                landed(y).wait_recv()
                for n in range(3):
                    pass_first(n).start()

    cholesky_body(piv, l_ref, i_ref, x_ref, after)

    @pl.when(c == 0)
    def _():
        for i in range(R):
            @pl.when(r == i)
            def _():
                for d in range(1, R):
                    pivot_copy(i, d).wait_send()
            pivot_hand(i, False).wait_send()
        for n in range(5):
            own_second(n).wait_send()

        @pl.when(r >= 4)
        def _():
            for n in range(5):
                own_high(n).wait_send()
            for n in range(3):
                pass_first(n).wait_send()

        @pl.when(r < 4)
        def _():
            for n in range(4):
                own_low(n).wait_send()
            keep_low.wait()

        for i in range(4):
            @pl.when(y != i)
            def _():
                landed(i).wait_recv()

        hand.wait_send()
        keep_panel.wait()
        for d in range(1, F):
            contrib_low(d).wait()
        inc_own_low.wait()

    @pl.when(c == 1)
    def _():
        hand.wait_recv()
        for i in range(4):
            @pl.when((y != i) | (r >= 4))
            def _():
                landed(i).wait_recv()
        for q in range(R):
            @pl.when(across != q)
            def _():
                landed(4 + q).wait_recv()
        for n in range(3):
            pass_second(n).wait_send()

        @pl.when(r < 4)
        def _():
            for n in range(3):
                pass_first(n).wait_send()

        for d in range(1, F):
            contrib_high(d).wait()
        inc_own_high.wait()


def exchange(front, contrib, dest, place, size):
    sm = pl.BlockSpec(memory_space=pltpu.SMEM)
    eight = pltpu.SemaphoreType.DMA((8,))
    one = pltpu.SemaphoreType.DMA
    return pl.pallas_call(
        exchange_kernel,
        out_shape=(
            jax.ShapeDtypeStruct((LB - 1, B, PC), F32),
            jax.ShapeDtypeStruct((12, B, PC), F32),
            jax.ShapeDtypeStruct((F, B, HW), F32),
            jax.ShapeDtypeStruct((F, 8, B), jnp.int32),
            jax.ShapeDtypeStruct((PC, PC), F32),
            jax.ShapeDtypeStruct((PC // KD, KD, KD), F32),
        ),
        in_specs=[ANY, ANY, sm, sm, sm],
        out_specs=(ANY, ANY, ANY, VM, VM, VM),
        scratch_shapes=[
            pltpu.VMEM((NB, B, B), F32),
            pltpu.VMEM((4, B, HW), F32),
            pltpu.VMEM((F, B, HW), F32),
            pltpu.VMEM((LB - 1, B, PC), F32),
            pltpu.VMEM((F, B, PC), F32),
            pltpu.VMEM((R, B, PC), F32),
            pltpu.VMEM((F, 8, B), jnp.int32),
            eight, eight, eight, eight, eight, eight, eight, eight, eight, one, one,
            pltpu.SemaphoreType.DMA((10,)),
            pltpu.SemaphoreType.DMA((12,)),
            pltpu.SemaphoreType.DMA((6,)),
            pltpu.SemaphoreType.DMA((6,)),
        ],
        compiler_params=pltpu.CompilerParams(collective_id=0, has_side_effects=True, vmem_limit_bytes=50 * MIB),
    )(front, contrib, dest, place, size)


def final_kernel(meta_ref, front_ref, inc_ref, panel_any, win_ref, l_ref, i_ref, out_ref, panel_ref, ph, plo, wh, wl, l3, sem):
    t = pl.program_id(0)
    col = meta_ref[1]
    steps = PC // KD

    def solve(blocks, source_ref, hi_ref, lo_ref, at):
        rows = blocks * B
        his, los = [], []
        for k in range(steps):
            cols = slice(k * KD, (k + 1) * KD)
            a = source_ref[pl.ds(at, blocks), :, cols].reshape(rows, KD)
            for m in range(k):
                a = a - dot_nt(
                    left3(his[m], los[m]), l3[cols, 3 * m * KD : 3 * (m + 1) * KD]
                )
            p = dot3(a, i_ref[k])
            hi, lo = split(p)
            his.append(hi)
            los.append(lo)
            hi_ref[pl.ds(at * B, rows), cols] = hi
            lo_ref[pl.ds(at * B, rows), cols] = lo

    @pl.when(t == 0)
    def _():
        pltpu.make_async_copy(panel_any, panel_ref, sem).start()

        for m in range(steps - 1):
            hi, lo = split(l_ref[:, m * KD : (m + 1) * KD])
            l3[:, 3 * m * KD : 3 * (m + 1) * KD] = right3(hi, lo)
        pltpu.make_async_copy(panel_any, panel_ref, sem).wait()
        solve(6, panel_ref, ph, plo, 0)
        solve(5, panel_ref, ph, plo, 6)
        solve(4, win_ref, wh, wl, 0)

        @pl.when(col == 1)
        def _():
            solve(4, win_ref, wh, wl, 4)
            solve(4, win_ref, wh, wl, 8)

    @pl.when((col == 0) & (t < steps))
    def _():
        row = pl.multiple_of(meta_ref[0] * B, B)
        for k in range(steps):
            @pl.when(t == k)
            def _():
                cols = slice(k * KD, (k + 1) * KD)
                out_ref[0] = l_ref[pl.ds(row, B), cols]
                out_ref[1:] = (ph[:, cols].astype(F32) + plo[:, cols].astype(F32)).reshape(LB - 1, B, KD)

    @pl.when((col == 1) | (t >= steps))
    def _():
        start = pl.multiple_of((t - jnp.where(col == 0, steps, 0)) * KD, KD)
        w_hi, w_lo = wh[pl.ds(start, KD), :], wl[pl.ds(start, KD), :]
        update = dot_nt(ph[...], w_hi) + dot_nt(plo[...], w_hi) + dot_nt(ph[...], w_lo)
        out_ref[0] = jnp.zeros((B, KD), F32)
        for lb in range(1, LB):
            valid = (lb * R + meta_ref[0]) * B < meta_ref[2]
            out_ref[lb] = jnp.where(valid, front_ref[lb], 0.0) - update[(lb - 1) * B : lb * B]
        for s in range(F):
            place = meta_ref[3 + s]

            @pl.when(place >= 0)
            def _():
                out_ref[pl.ds(place, 1)] += inc_ref[s : s + 1]


def final(meta, front, inc, panel, win, low, inv):
    tiles = HW // KD
    whole = dict(pipeline_mode=pl.Buffered(1))
    return pl.pallas_call(
        final_kernel,
        grid_spec=pltpu.PrefetchScalarGridSpec(
            num_scalar_prefetch=1,
            grid=(tiles,),
            in_specs=[
                pl.BlockSpec((LB, B, KD), lambda t, meta: (0, 0, t)),
                pl.BlockSpec((F, B, KD), lambda t, meta: (0, 0, t)),
                ANY,
                pl.BlockSpec((12, B, PC), lambda t, meta: (0, 0, 0), **whole),
                pl.BlockSpec((PC, PC), lambda t, meta: (0, 0), **whole),
                pl.BlockSpec((PC // KD, KD, KD), lambda t, meta: (0, 0, 0), **whole),
            ],
            out_specs=pl.BlockSpec((LB, B, KD), lambda t, meta: (0, 0, t)),
            scratch_shapes=[
                pltpu.VMEM((LB - 1, B, PC), F32),
                pltpu.VMEM(((LB - 1) * B, PC), jnp.bfloat16),
                pltpu.VMEM(((LB - 1) * B, PC), jnp.bfloat16),
                pltpu.VMEM((12 * B, PC), jnp.bfloat16),
                pltpu.VMEM((12 * B, PC), jnp.bfloat16),
                pltpu.VMEM((PC, 3 * (PC - KD)), jnp.bfloat16),
                pltpu.SemaphoreType.DMA,
            ],
        ),
        out_shape=jax.ShapeDtypeStruct((LB, B, HW), F32),
        compiler_params=pltpu.CompilerParams(vmem_limit_bytes=60 * MIB),
    )(meta, front, inc, panel, win, low, inv)


def on_device(front_matrix, front_sizes, contrib, dest_front, dest_local):
    front = front_matrix[0]
    panel, win, inc, got, low, inv = exchange(front, contrib[0], dest_front[0, :, 0], dest_local[0, :, 0], front_sizes)
    row_col = jnp.stack([lax.axis_index("row"), lax.axis_index("col"), front_sizes[0]]).astype(jnp.int32)
    meta = jnp.concatenate([row_col, got[:, 0, 0]])
    out = final(meta, front, inc, panel, win, low, inv)
    return out[None]


def solution(mesh):
    return jax.shard_map(
        on_device,
        mesh=mesh,
        in_specs=(
            P("front", None, "row", "col"),
            P("front"),
            P("front", None, "row", "col"),
            P("front", None, "row"),
            P("front", None, "row"),
        ),
        out_specs=P("front", None, "row", "col"),
        check_vma=False,
    )
```

```python
import functools

import jax
import jax.numpy as jnp
from jax import lax
from jax.experimental import pallas as pl
from jax.experimental.pallas import tpu as pltpu
from jax.sharding import PartitionSpec as P

F = 8
R = 8
B = 128
LB = 12
HW = 1536
PC = 1024
NB = PC // B
PW = 512
KD = 256
KA = (1, 3)
KC = 0
KF = (3, 6)
MESH = pl.DeviceIdType.MESH
ANY = pl.BlockSpec(memory_space=pl.ANY)
VM = pl.BlockSpec(memory_space=pltpu.VMEM)
F32 = jnp.float32
BF16 = jnp.bfloat16
MIB = 2**20


def split(x):
    hi = x.astype(jnp.bfloat16)
    return hi, (x - hi.astype(F32)).astype(jnp.bfloat16)


def left3(hi, lo):
    return jnp.concatenate([hi, lo, hi], 1)


def right3(hi, lo):
    return jnp.concatenate([hi, hi, lo], 1)


def dot_nt(a, b):
    return lax.dot_general(a, b, (((1,), (1,)), ((), ())), preferred_element_type=F32)


def dot_nn(a, b):
    return lax.dot_general(a, b, (((1,), (0,)), ((), ())), preferred_element_type=F32)


def dot3(a, b):
    return dot_nt(left3(*split(a)), right3(*split(b)))


def dot3_nn(a, b):
    bh, bl = split(b)
    return dot_nn(left3(*split(a)), jnp.concatenate([bh, bh, bl], 0))


def recip(x):
    first = pl.reciprocal(x, approx=True)
    return first * (2.0 - x * first)


def lane_spread(x, k):
    return jnp.broadcast_to(x[:, k : k + 1], (8, B))


def row_spread(x, j):
    return jnp.broadcast_to(x[j : j + 1, :], (8, B))


def factor_block(sym):
    sub = lax.broadcasted_iota(jnp.int32, (8, B), 0)
    lane = lax.broadcasted_iota(jnp.int32, (8, B), 1)
    count = B // 8
    rows = [sym[q * 8 : (q + 1) * 8, :] for q in range(count)]
    eyes = [jnp.where(lane == sub + q * 8, 1.0, 0.0).astype(F32) for q in range(count)]
    factor, inverse = [], []
    for p in range(count):
        v, e = rows[p], eyes[p]
        c = [lane_spread(v, p * 8 + k) for k in range(8)]
        more = p < count - 1
        if more:
            v2, e2 = rows[p + 1], eyes[p + 1]
            c2 = [lane_spread(v2, p * 8 + k) for k in range(8)]
        diagonal = None
        for j in range(8):
            pivot = row_spread(c[j], j)
            diagonal = pivot if diagonal is None else jnp.where(sub == j, pivot, diagonal)
            over = recip(pivot)
            rv, re = row_spread(v, j), row_spread(e, j)
            m = jnp.where(sub > j, c[j] * over, 0.0)
            if more:
                m2 = c2[j] * over
            for k in range(j + 1, 8):
                s = row_spread(c[k], j)
                c[k] = c[k] - m * s
                if more:
                    c2[k] = c2[k] - m2 * s
            v = v - m * rv
            e = e - m * re
            if more:
                v2 = v2 - m2 * rv
                e2 = e2 - m2 * re
        scale = lax.rsqrt(diagonal)
        factor.append(jnp.where(lane >= sub + p * 8, v * scale, 0.0))
        inverse.append(e * scale)
        if more:
            rows[p + 1], eyes[p + 1] = v2, e2
        if p < count - 2:
            t = (v * recip(diagonal)).T
            rv = [row_spread(v, j) for j in range(8)]
            re = [row_spread(e, j) for j in range(8)]
            for q in range(p + 2, count):
                tq = t[q * 8 : (q + 1) * 8, :]
                for j in range(8):
                    m = jnp.broadcast_to(tq[:, j : j + 1], (8, B))
                    rows[q] = rows[q] - m * rv[j]
                    eyes[q] = eyes[q] - m * re[j]
    return jnp.concatenate(factor, 0), jnp.concatenate(inverse, 0)


def cholesky_body(a_ref, l_ref, i_ref, x_ref, lh, ll, after):
    row_id = lax.broadcasted_iota(jnp.int32, (B, B), 0)
    col_id = lax.broadcasted_iota(jnp.int32, (B, B), 1)

    def step(k, carry):
        def owed(kk):
            def run():
                o = kk * B
                a = a_ref[kk:, :, o : o + B].reshape(PC - o, B)
                if kk > 0:
                    mine_h, mine_l = lh[o : o + B, :o], ll[o : o + B, :o]
                    a = a - (dot_nt(lh[o:, :o], mine_h) + dot_nt(ll[o:, :o], mine_h) + dot_nt(lh[o:, :o], mine_l))
                l_ref[o:, o : o + B] = a

            return run

        for kk in range(NB):
            pl.when(k == kk)(owed(kk))
        o = pl.multiple_of(k * B, B)
        d = l_ref[pl.ds(o, B), pl.ds(o, B)]
        lt, li = factor_block(jnp.where(row_id >= col_id, d, d.T))
        l_ref[pl.ds(o, B), pl.ds(o, B)] = lt.T
        x_ref[k] = li

        def below(kk):
            def run():
                base = (kk + 1) * B
                x = dot3(l_ref[base:, kk * B : base], li)
                l_ref[base:, kk * B : base] = x
                lh[base:, kk * B : base], ll[base:, kk * B : base] = split(x)

            return run

        for kk in range(NB - 1):
            pl.when(k == kk)(below(kk))
        after(k)
        return carry

    lax.fori_loop(0, NB, step, 0)
    for i in range(NB - 1):
        l_ref[i * B : (i + 1) * B, (i + 1) * B :] = jnp.zeros((B, (NB - 1 - i) * B), F32)
    for i in range(NB // 2):
        low, high = x_ref[2 * i], x_ref[2 * i + 1]
        between = l_ref[(2 * i + 1) * B : (2 * i + 2) * B, 2 * i * B : (2 * i + 1) * B]
        i_ref[i, :B, :B] = low
        i_ref[i, :B, B:] = jnp.zeros((B, B), F32)
        i_ref[i, B:, :B] = -dot3_nn(high, dot3_nn(between, low))
        i_ref[i, B:, B:] = high


def exchange_kernel(
    front_ref, contrib_ref, dest_ref, local_ref, size_ref,
    ph_ref, plo_ref, wh_ref, wl_ref, inc_ref, got_ref, l_ref,
    i_ref, x_ref, lh, ll, cont, packed, pan, win_ref, inc_p, piv, place_v, ph, plo, wh, wl,
    psend, precv, fsend, qsend, qrecv, rsend, asend, arecv, bsend, brecv, lsend, lrecv, hsend, hrecv, wsend, wrecv, gsend, local, outs,
):
    f = lax.axis_index("front")
    r = lax.axis_index("row")
    c = lax.axis_index("col")
    y = lax.rem(r, 4)
    side = r - y
    across = lax.rem(r + 4, R)
    rest = HW - PC

    load_contrib = pltpu.make_async_copy(contrib_ref, cont, local.at[0])
    load_contrib.start()
    load_panel = pltpu.make_async_copy(front_ref.at[pl.ds(1, LB - 1), :, pl.ds(0, PC)], pan, local.at[1])

    @pl.when(c == 0)
    def _():
        load_panel.start()

    barrier = pltpu.get_barrier_semaphore()
    for d in range(1, F):
        pl.semaphore_signal(barrier, inc=1, device_id={"front": lax.rem(f + d, F)}, device_id_type=MESH)
        pl.semaphore_signal(barrier, inc=1, device_id={"row": lax.rem(r + d, R)}, device_id_type=MESH)
    for d in range(R):
        pl.semaphore_signal(barrier, inc=1, device_id={"row": lax.rem(r + d, R), "col": 1 - c}, device_id_type=MESH)
    pl.semaphore_wait(barrier, F - 1 + R - 1 + R)

    def send(src, dst, send_sem, recv_sem, **device):
        return pltpu.make_async_remote_copy(
            src_ref=src, dst_ref=dst, send_sem=send_sem, recv_sem=recv_sem, device_id=device, device_id_type=MESH
        )

    near = (1, 3, 2)

    def row_at(d):
        return side + lax.rem(y + d, 4)

    def part(i, late):
        return pl.ds(KD, (i - 1) * B) if late else pl.ds(0, KD)

    def pivot_copy(i, n, late):
        cols = part(i, late)
        ss, rs = (qsend, qrecv) if late else (psend, precv)
        row = across if n == 0 else row_at(near[n - 1])
        return send(front_ref.at[0, :, cols], piv.at[i, :, cols], ss.at[n], rs.at[i], row=row)

    def pivot_pass(i, n, late):
        cols = part(i, late)
        ss, rs = (qsend, qrecv) if late else (psend, precv)
        return send(piv.at[i, :, cols], piv.at[i, :, cols], ss.at[4 + n], rs.at[i], row=row_at(near[n]))

    def pivot_own(i):
        cols = pl.ds(0, max(i + 1, 2) * B)
        return pltpu.make_async_copy(front_ref.at[0, :, cols], piv.at[i, :, cols], local.at[2])

    def pivot_hand(i, own, late):
        cols = part(i, late)
        ss, rs = (rsend, qrecv) if late else (fsend, precv)
        src = front_ref.at[0, :, cols] if own else piv.at[i, :, cols]
        return send(src, piv.at[i, :, cols], ss.at[i], rs.at[i], col=1)

    @pl.when(c == 0)
    def _():
        for late in (False, True):
            for i in range(2 if late else 0, R):
                @pl.when(r == i)
                def _():
                    for n in range(4):
                        pivot_copy(i, n, late).start()
                    pivot_hand(i, True, late).start()
                    if not late:
                        pivot_own(i).start()

    def hand_on(late):
        order = [across] + [row_at(d) for d in near] + [(4 - side) + lax.rem(y + d, 4) for d in near]
        for at, row in enumerate(order):
            for i in range(2 if late else 0, R):
                @pl.when(row == i)
                def _():
                    pivot_hand(i, False, late).wait_recv()
                    if at == 0:
                        for n in range(3):
                            pivot_pass(i, n, late).start()
                    pivot_hand(i, False, late).start()

    def contrib_panel(d, h):
        to = lax.rem(f + d, F)
        cols = pl.ds(h * PW, PW)
        return send(packed.at[to, :, cols], inc_p.at[f, :, cols], asend.at[h, d], arecv.at[h, d], front=to)

    def contrib_low(d):
        to = lax.rem(f + d, F)
        cols = pl.ds(PC, rest)
        return send(packed.at[to, :, cols], inc_ref.at[f, :, cols], bsend.at[d], brecv.at[d], front=to)

    def contrib_high(d):
        to = lax.rem(f + d, F)
        return send(packed.at[to], inc_ref.at[f], bsend.at[d], brecv.at[d], front=to)

    def place_copy(d):
        to = lax.rem(f + d, F)
        return send(place_v.at[to], got_ref.at[f], lsend.at[d], lrecv.at[d], front=to)

    def choice(to):
        which, place = 0, -1
        for k in range(4):
            mine = dest_ref[k] == to
            which = jnp.where(mine, k, which)
            place = jnp.where(mine, local_ref[k], place)
        return which, place

    load_contrib.wait()

    @pl.when(c == 0)
    def _():
        def one(d, carry):
            to = lax.rem(f + d, F)
            which, _ = choice(to)
            packed[to, :, :PC] = cont[which, :, :PC]
            contrib_panel(d, 0).start()
            return carry

        lax.fori_loop(1, F, one, 0)
        for d in range(1, F):
            contrib_panel(d, 1).start()
        which, _ = choice(f)
        inc_p[f] = cont[which, :, :PC]

    def place_one(d, carry):
        to = lax.rem(f + d, F)
        _, place = choice(to)
        place_v[to] = jnp.full((8, B), place, jnp.int32)
        place_copy(d).start()
        return carry

    lax.fori_loop(1, F, place_one, 0)
    _, own_place = choice(f)
    got_ref[f] = jnp.full((8, B), own_place, jnp.int32)

    def pack_low(d, carry):
        to = lax.rem(f + d, F)
        which, _ = choice(to)
        packed[to, :, PC:] = cont[which, :, PC:]
        return carry

    def pack_high(d, carry):
        to = lax.rem(f + d, F)
        which, _ = choice(to)
        packed[to] = cont[which]
        return carry

    @pl.when(c == 0)
    def _():
        lax.fori_loop(0, F, pack_low, 0)

    @pl.when(c == 1)
    def _():
        lax.fori_loop(0, F, pack_high, 0)

    inc_own_low = pltpu.make_async_copy(packed.at[f, :, pl.ds(PC, rest)], inc_ref.at[f, :, pl.ds(PC, rest)], local.at[3])
    inc_own_high = pltpu.make_async_copy(packed.at[f], inc_ref.at[f], local.at[3])

    for d in range(1, F):
        place_copy(d).wait()

    @pl.when(c == 0)
    def _():
        hand_on(False)
        for i in range(R):
            @pl.when(r == i)
            def _():
                pivot_own(i).wait()

    @pl.when(c == 1)
    def _():
        for i in range(R):
            pivot_hand(i, False, False).wait_recv()

    def half_of(h):
        return pl.ds(h * PW, PW)

    def own_second(n, h):
        cols = half_of(h)
        src, dst, ss, rs = pan.at[1, :, cols], win_ref.at[4 + r, :, cols], wsend.at[h, n], wrecv.at[h, 4 + r]
        if n == 0:
            return send(src, dst, ss, rs, row=across, col=1)
        if n == 1:
            return send(src, dst, ss, rs, col=1)
        return send(src, dst, ss, rs, row=row_at(near[n - 2]), col=1)

    def own_high(n, h):
        cols = half_of(h)
        src, dst, ss, rs = pan.at[0, :, cols], win_ref.at[r - 4, :, cols], wsend.at[h, 5 + n], wrecv.at[h, r - 4]
        if n == 0:
            return send(src, dst, ss, rs, row=across, col=1)
        if n == 1:
            return send(src, dst, ss, rs, col=1)
        return send(src, dst, ss, rs, row=row_at(near[n - 2]), col=1)

    def own_low(n, h):
        cols = half_of(h)
        src, dst, ss, rs = pan.at[0, :, cols], win_ref.at[r, :, cols], wsend.at[h, 5 + n], wrecv.at[h, r]
        if n == 0:
            return send(src, dst, ss, rs, row=across)
        return send(src, dst, ss, rs, row=row_at(near[n - 1]))

    keep_low = pltpu.make_async_copy(pan.at[0], win_ref.at[y], local.at[4])
    hand = send(pan, pan, hsend, hrecv, col=1)

    def landed(i, h):
        cols = half_of(h)
        return send(pan.at[0, :, cols], win_ref.at[i, :, cols], gsend.at[h, 0], wrecv.at[h, i], col=1 - c)

    def landed_all(i):
        for h in range(2):
            landed(i, h).wait_recv()

    def pass_second(n, h):
        here = win_ref.at[4 + across, :, half_of(h)]
        return send(here, here, gsend.at[h, n], wrecv.at[h, 4 + across], row=row_at(near[n]))

    def pass_first(n, h):
        here = win_ref.at[y, :, half_of(h)]
        return send(here, here, gsend.at[h, 3 + n], wrecv.at[h, y], row=row_at(near[n]))

    def assemble(lb, h):
        valid = (lb * R + r) * B < size_ref[0]
        cols = slice(h * PW, (h + 1) * PW)

        def eight(i, carry):
            at = pl.ds(pl.multiple_of(i * 8, 8), 8)
            total = jnp.where(valid, pan[lb - 1, at, cols], 0.0)
            for s in range(F):
                mask = jnp.concatenate([got_ref[s]] * (PW // B), 1) == lb
                total = total + jnp.where(mask, inc_p[s, at, cols], 0.0)
            pan[lb - 1, at, cols] = total
            return carry

        lax.fori_loop(0, B // 8, eight, 0)

    def after(k):
        @pl.when((k == 0) & (c == 0))
        def _():
            hand_on(True)

        @pl.when((k == 1) & (c == 1))
        def _():
            for i in range(2, R):
                pivot_hand(i, False, True).wait_recv()

        for h in range(2):
            @pl.when((k == KA[h]) & (c == 0))
            def _():
                if h == 0:
                    load_panel.wait()
                for d in range(1, F):
                    contrib_panel(d, h).wait()
                assemble(2, h)
                for n in range(5):
                    own_second(n, h).start()
                assemble(1, h)

                @pl.when(r >= 4)
                def _():
                    for n in range(5):
                        own_high(n, h).start()

                @pl.when(r < 4)
                def _():
                    for n in range(4):
                        own_low(n, h).start()
                    if h == 1:
                        keep_low.start()

                if h == 1:
                    for d in range(1, F):
                        contrib_low(d).start()
                    inc_own_low.start()

                def others(lb, carry):
                    assemble(lb, h)
                    return carry

                lax.fori_loop(3, LB, others, 0)
                if h == 1:
                    hand.start()

        @pl.when((k == KC) & (c == 1))
        def _():
            for d in range(1, F):
                contrib_high(d).start()
            inc_own_high.start()

        for h in range(2):
            @pl.when((k == KF[h]) & (c == 0) & (r >= 4))
            def _():
                landed(y, h).wait_recv()
                for n in range(3):
                    pass_first(n, h).start()

            @pl.when((k == KF[h]) & (c == 1))
            def _():
                landed(4 + across, h).wait_recv()
                for n in range(3):
                    pass_second(n, h).start()

                @pl.when(r < 4)
                def _():
                    landed(y, h).wait_recv()
                    for n in range(3):
                        pass_first(n, h).start()

    cholesky_body(piv, l_ref, i_ref, x_ref, lh, ll, after)

    def solve(source, hi_ref, lo_ref, at, blocks):
        rows = slice(at * B, (at + blocks) * B)
        for k in range(PC // KD):
            o = k * KD
            cols = slice(o, o + KD)
            a = source[at : at + blocks, :, cols].reshape(blocks * B, KD)
            if k > 0:
                mine_h, mine_l = lh[cols, :o], ll[cols, :o]
                hi, lo = hi_ref[rows, :o], lo_ref[rows, :o]
                a = a - (dot_nt(hi, mine_h) + dot_nt(lo, mine_h) + dot_nt(hi, mine_l))
            hi_ref[rows, cols], lo_ref[rows, cols] = split(dot3(a, i_ref[k]))

    def out_copy(n, low):
        at = pl.ds(0, 4 * B) if low else pl.ds(0, 12 * B)
        pairs = ((ph, ph_ref), (plo, plo_ref), (wh.at[at], wh_ref.at[at]), (wl.at[at], wl_ref.at[at]))
        return pltpu.make_async_copy(*pairs[n], outs.at[n])

    @pl.when(c == 1)
    def _():
        hand.wait_recv()

    solve(pan, ph, plo, 0, 6)
    solve(pan, ph, plo, 6, 5)
    out_copy(0, False).start()
    out_copy(1, False).start()

    @pl.when(c == 0)
    def _():
        @pl.when(r < 4)
        def _():
            keep_low.wait()

        for i in range(4):
            @pl.when(y != i)
            def _():
                landed_all(i)

        solve(win_ref, wh, wl, 0, 4)
        out_copy(2, True).start()
        out_copy(3, True).start()

    @pl.when(c == 1)
    def _():
        for i in range(4):
            @pl.when((y != i) | (r >= 4))
            def _():
                landed_all(i)
        solve(win_ref, wh, wl, 0, 4)
        for half in range(2):
            for q in range(4 * half, 4 * half + 4):
                @pl.when(across != q)
                def _():
                    landed_all(4 + q)
            solve(win_ref, wh, wl, 4 * (half + 1), 4)
        out_copy(2, False).start()
        out_copy(3, False).start()

    @pl.when(c == 0)
    def _():
        for i in range(R):
            @pl.when(r == i)
            def _():
                for n in range(4):
                    pivot_copy(i, n, False).wait_send()
                    if i >= 2:
                        pivot_copy(i, n, True).wait_send()

            @pl.when(across == i)
            def _():
                for n in range(3):
                    pivot_pass(i, n, False).wait_send()
                    if i >= 2:
                        pivot_pass(i, n, True).wait_send()

            pivot_hand(i, False, False).wait_send()
            if i >= 2:
                pivot_hand(i, False, True).wait_send()
        for n in range(5):
            for h in range(2):
                own_second(n, h).wait_send()

        @pl.when(r >= 4)
        def _():
            for n in range(5):
                for h in range(2):
                    own_high(n, h).wait_send()
            for n in range(3):
                for h in range(2):
                    pass_first(n, h).wait_send()

        @pl.when(r < 4)
        def _():
            for n in range(4):
                for h in range(2):
                    own_low(n, h).wait_send()

        hand.wait_send()
        for d in range(1, F):
            contrib_low(d).wait()
        inc_own_low.wait()
        out_copy(2, True).wait()
        out_copy(3, True).wait()

    @pl.when(c == 1)
    def _():
        for n in range(3):
            for h in range(2):
                pass_second(n, h).wait_send()

        @pl.when(r < 4)
        def _():
            for n in range(3):
                for h in range(2):
                    pass_first(n, h).wait_send()

        for d in range(1, F):
            contrib_high(d).wait()
        inc_own_high.wait()
        out_copy(2, False).wait()
        out_copy(3, False).wait()

    out_copy(0, False).wait()
    out_copy(1, False).wait()


def exchange(front, contrib, dest, place, size):
    sm = pl.BlockSpec(memory_space=pltpu.SMEM)
    eight = pltpu.SemaphoreType.DMA((8,))
    one = pltpu.SemaphoreType.DMA
    own = ((LB - 1) * B, PC)
    window = (12 * B, PC)
    return pl.pallas_call(
        exchange_kernel,
        out_shape=(
            jax.ShapeDtypeStruct(own, BF16),
            jax.ShapeDtypeStruct(own, BF16),
            jax.ShapeDtypeStruct(window, BF16),
            jax.ShapeDtypeStruct(window, BF16),
            jax.ShapeDtypeStruct((F, B, HW), F32),
            jax.ShapeDtypeStruct((F, 8, B), jnp.int32),
            jax.ShapeDtypeStruct((PC, PC), F32),
        ),
        in_specs=[ANY, ANY, sm, sm, sm],
        out_specs=(ANY, ANY, ANY, ANY, ANY, VM, VM),
        scratch_shapes=[
            pltpu.VMEM((PC // KD, KD, KD), F32),
            pltpu.VMEM((NB, B, B), F32),
            pltpu.VMEM((PC, PC), BF16),
            pltpu.VMEM((PC, PC), BF16),
            pltpu.VMEM((4, B, HW), F32),
            pltpu.VMEM((F, B, HW), F32),
            pltpu.VMEM((LB - 1, B, PC), F32),
            pltpu.VMEM((12, B, PC), F32),
            pltpu.VMEM((F, B, PC), F32),
            pltpu.VMEM((R, B, PC), F32),
            pltpu.VMEM((F, 8, B), jnp.int32),
            pltpu.VMEM(own, BF16),
            pltpu.VMEM(own, BF16),
            pltpu.VMEM(window, BF16),
            pltpu.VMEM(window, BF16),
            eight,
            eight,
            eight,
            eight,
            eight,
            eight,
            pltpu.SemaphoreType.DMA((2, 8)),
            pltpu.SemaphoreType.DMA((2, 8)),
            eight,
            eight,
            eight,
            eight,
            one,
            one,
            pltpu.SemaphoreType.DMA((2, 10)),
            pltpu.SemaphoreType.DMA((2, 12)),
            pltpu.SemaphoreType.DMA((2, 6)),
            pltpu.SemaphoreType.DMA((6,)),
            pltpu.SemaphoreType.DMA((4,)),
        ],
        compiler_params=pltpu.CompilerParams(collective_id=0, has_side_effects=True, vmem_limit_bytes=62 * MIB),
    )(front, contrib, dest, place, size)


def final_kernel(meta_ref, front_ref, inc_ref, l_ref, ph, plo, wh, wl, out_ref):
    t = pl.program_id(0)
    col = meta_ref[1]
    steps = PC // KD

    @pl.when((col == 0) & (t < steps))
    def _():
        for k in range(steps):
            @pl.when(t == k)
            def _():
                cols = slice(k * KD, (k + 1) * KD)
                out_ref[0] = l_ref[:, cols]
                out_ref[1:] = (ph[:, cols].astype(F32) + plo[:, cols].astype(F32)).reshape(LB - 1, B, KD)

    @pl.when((col == 1) | (t >= steps))
    def _():
        start = pl.multiple_of((t - jnp.where(col == 0, steps, 0)) * KD, KD)
        w_hi, w_lo = wh[pl.ds(start, KD), :], wl[pl.ds(start, KD), :]
        update = dot_nt(ph[...], w_hi) + dot_nt(plo[...], w_hi) + dot_nt(ph[...], w_lo)
        out_ref[0] = jnp.zeros((B, KD), F32)
        for lb in range(1, LB):
            valid = (lb * R + meta_ref[0]) * B < meta_ref[2]
            out_ref[lb] = jnp.where(valid, front_ref[lb], 0.0) - update[(lb - 1) * B : lb * B]
        for s in range(F):
            place = meta_ref[3 + s]

            @pl.when(place >= 0)
            def _():
                out_ref[pl.ds(place, 1)] += inc_ref[s : s + 1]


def final(meta, front, inc, low, solved):
    tiles = HW // KD
    whole = dict(pipeline_mode=pl.Buffered(1))
    return pl.pallas_call(
        final_kernel,
        grid_spec=pltpu.PrefetchScalarGridSpec(
            num_scalar_prefetch=1,
            grid=(tiles,),
            in_specs=[
                pl.BlockSpec((LB, B, KD), lambda t, meta: (0, 0, t)),
                pl.BlockSpec((F, B, KD), lambda t, meta: (0, 0, t)),
                pl.BlockSpec((B, PC), lambda t, meta: (meta[0], 0), **whole),
                pl.BlockSpec(((LB - 1) * B, PC), lambda t, meta: (0, 0), **whole),
                pl.BlockSpec(((LB - 1) * B, PC), lambda t, meta: (0, 0), **whole),
                pl.BlockSpec((12 * B, PC), lambda t, meta: (0, 0), **whole),
                pl.BlockSpec((12 * B, PC), lambda t, meta: (0, 0), **whole),
            ],
            out_specs=pl.BlockSpec((LB, B, KD), lambda t, meta: (0, 0, t)),
        ),
        out_shape=jax.ShapeDtypeStruct((LB, B, HW), F32),
        compiler_params=pltpu.CompilerParams(vmem_limit_bytes=60 * MIB),
    )(meta, front, inc, low, *solved)


def on_device(front_matrix, front_sizes, contrib, dest_front, dest_local):
    front = front_matrix[0]
    *solved, inc, got, low = exchange(front, contrib[0], dest_front[0, :, 0], dest_local[0, :, 0], front_sizes)
    row_col = jnp.stack([lax.axis_index("row"), lax.axis_index("col"), front_sizes[0]]).astype(jnp.int32)
    meta = jnp.concatenate([row_col, got[:, 0, 0]])
    out = final(meta, front, inc, low, solved)
    return out[None]


def solution(mesh):
    return jax.shard_map(
        on_device,
        mesh=mesh,
        in_specs=(
            P("front", None, "row", "col"),
            P("front"),
            P("front", None, "row", "col"),
            P("front", None, "row"),
            P("front", None, "row"),
        ),
        out_specs=P("front", None, "row", "col"),
        check_vma=False,
    )
```

```python
import functools

import jax
import jax.numpy as jnp
from jax import lax
from jax.experimental import pallas as pl
from jax.experimental.pallas import tpu as pltpu
from jax.sharding import PartitionSpec as P

F = 8
R = 8
B = 128
LB = 12
HW = 1536
PC = 1024
NB = PC // B
PW = 512
KD = 256
KA = (1, 3)
KC = 3
KF = (3, 6)
MESH = pl.DeviceIdType.MESH
ANY = pl.BlockSpec(memory_space=pl.ANY)
VM = pl.BlockSpec(memory_space=pltpu.VMEM)
F32 = jnp.float32
BF16 = jnp.bfloat16
MIB = 2**20


def split(x):
    hi = x.astype(jnp.bfloat16)
    return hi, (x - hi.astype(F32)).astype(jnp.bfloat16)


def left3(hi, lo):
    return jnp.concatenate([hi, lo, hi], 1)


def right3(hi, lo):
    return jnp.concatenate([hi, hi, lo], 1)


def dot_nt(a, b):
    return lax.dot_general(a, b, (((1,), (1,)), ((), ())), preferred_element_type=F32)


def dot_nn(a, b):
    return lax.dot_general(a, b, (((1,), (0,)), ((), ())), preferred_element_type=F32)


def dot3(a, b):
    return dot_nt(left3(*split(a)), right3(*split(b)))


def dot3_nn(a, b):
    bh, bl = split(b)
    return dot_nn(left3(*split(a)), jnp.concatenate([bh, bh, bl], 0))


def recip(x):
    first = pl.reciprocal(x, approx=True)
    return first * (2.0 - x * first)


def lane_spread(x, k):
    return jnp.broadcast_to(x[:, k : k + 1], (8, B))


def row_spread(x, j):
    return jnp.broadcast_to(x[j : j + 1, :], (8, B))


def factor_block(sym):
    sub = lax.broadcasted_iota(jnp.int32, (8, B), 0)
    lane = lax.broadcasted_iota(jnp.int32, (8, B), 1)
    count = B // 8
    rows = [sym[q * 8 : (q + 1) * 8, :] for q in range(count)]
    eyes = [jnp.where(lane == sub + q * 8, 1.0, 0.0).astype(F32) for q in range(count)]
    factor, inverse = [], []
    for p in range(count):
        v, e = rows[p], eyes[p]
        c = [lane_spread(v, p * 8 + k) for k in range(8)]
        more = p < count - 1
        if more:
            v2, e2 = rows[p + 1], eyes[p + 1]
            c2 = [lane_spread(v2, p * 8 + k) for k in range(8)]
        diagonal = None
        for j in range(8):
            pivot = row_spread(c[j], j)
            diagonal = pivot if diagonal is None else jnp.where(sub == j, pivot, diagonal)
            over = recip(pivot)
            rv, re = row_spread(v, j), row_spread(e, j)
            m = jnp.where(sub > j, c[j] * over, 0.0)
            if more:
                m2 = c2[j] * over
            for k in range(j + 1, 8):
                s = row_spread(c[k], j)
                c[k] = c[k] - m * s
                if more:
                    c2[k] = c2[k] - m2 * s
            v = v - m * rv
            e = e - m * re
            if more:
                v2 = v2 - m2 * rv
                e2 = e2 - m2 * re
        scale = lax.rsqrt(diagonal)
        factor.append(jnp.where(lane >= sub + p * 8, v * scale, 0.0))
        inverse.append(e * scale)
        if more:
            rows[p + 1], eyes[p + 1] = v2, e2
        if p < count - 2:
            t = (v * recip(diagonal)).T
            rv = [row_spread(v, j) for j in range(8)]
            re = [row_spread(e, j) for j in range(8)]
            for q in range(p + 2, count):
                tq = t[q * 8 : (q + 1) * 8, :]
                for j in range(8):
                    m = jnp.broadcast_to(tq[:, j : j + 1], (8, B))
                    rows[q] = rows[q] - m * rv[j]
                    eyes[q] = eyes[q] - m * re[j]
    return jnp.concatenate(factor, 0), jnp.concatenate(inverse, 0)


def cholesky_body(a_ref, l_ref, i_ref, x_ref, lh, ll, after):
    row_id = lax.broadcasted_iota(jnp.int32, (B, B), 0)
    col_id = lax.broadcasted_iota(jnp.int32, (B, B), 1)

    def step(k, carry):
        def owed(kk):
            def run():
                o = kk * B
                a = a_ref[kk:, :, o : o + B].reshape(PC - o, B)
                if kk > 0:
                    mine_h, mine_l = lh[o : o + B, :o], ll[o : o + B, :o]
                    a = a - (dot_nt(lh[o:, :o], mine_h) + dot_nt(ll[o:, :o], mine_h) + dot_nt(lh[o:, :o], mine_l))
                l_ref[o:, o : o + B] = a

            return run

        for kk in range(NB):
            pl.when(k == kk)(owed(kk))
        o = pl.multiple_of(k * B, B)
        d = l_ref[pl.ds(o, B), pl.ds(o, B)]
        lt, li = factor_block(jnp.where(row_id >= col_id, d, d.T))
        l_ref[pl.ds(o, B), pl.ds(o, B)] = lt.T
        x_ref[k] = li

        def below(kk):
            def run():
                base = (kk + 1) * B
                x = dot3(l_ref[base:, kk * B : base], li)
                l_ref[base:, kk * B : base] = x
                lh[base:, kk * B : base], ll[base:, kk * B : base] = split(x)

            return run

        for kk in range(NB - 1):
            pl.when(k == kk)(below(kk))
        after(k)
        return carry

    lax.fori_loop(0, NB, step, 0)
    for i in range(NB - 1):
        l_ref[i * B : (i + 1) * B, (i + 1) * B :] = jnp.zeros((B, (NB - 1 - i) * B), F32)
    for i in range(NB // 2):
        low, high = x_ref[2 * i], x_ref[2 * i + 1]
        between = l_ref[(2 * i + 1) * B : (2 * i + 2) * B, 2 * i * B : (2 * i + 1) * B]
        i_ref[i, :B, :B] = low
        i_ref[i, :B, B:] = jnp.zeros((B, B), F32)
        i_ref[i, B:, :B] = -dot3_nn(high, dot3_nn(between, low))
        i_ref[i, B:, B:] = high


def exchange_kernel(
    front_ref, contrib_ref, dest_ref, local_ref, size_ref,
    ph_ref, plo_ref, wh_ref, wl_ref, inc_ref, got_ref, l_ref,
    i_ref, x_ref, lh, ll, cont, packed, pan, win_ref, inc_p, piv, place_v, ph, plo, wh, wl,
    psend, precv, fsend, qsend, qrecv, rsend, asend, arecv, bsend, brecv, lsend, lrecv, hsend, hrecv, wsend, wrecv, gsend, local, outs,
):
    f = lax.axis_index("front")
    r = lax.axis_index("row")
    c = lax.axis_index("col")
    y = lax.rem(r, 4)
    side = r - y
    across = lax.rem(r + 4, R)
    rest = HW - PC

    load_contrib = pltpu.make_async_copy(contrib_ref, cont, local.at[0])
    load_contrib.start()
    load_panel = pltpu.make_async_copy(front_ref.at[pl.ds(1, LB - 1), :, pl.ds(0, PC)], pan, local.at[1])

    @pl.when(c == 0)
    def _():
        load_panel.start()

    barrier = pltpu.get_barrier_semaphore()
    for d in range(1, F):
        pl.semaphore_signal(barrier, inc=1, device_id={"front": lax.rem(f + d, F)}, device_id_type=MESH)
        pl.semaphore_signal(barrier, inc=1, device_id={"row": lax.rem(r + d, R)}, device_id_type=MESH)
    for d in range(R):
        pl.semaphore_signal(barrier, inc=1, device_id={"row": lax.rem(r + d, R), "col": 1 - c}, device_id_type=MESH)
    pl.semaphore_wait(barrier, F - 1 + R - 1 + R)

    def send(src, dst, send_sem, recv_sem, **device):
        return pltpu.make_async_remote_copy(
            src_ref=src, dst_ref=dst, send_sem=send_sem, recv_sem=recv_sem, device_id=device, device_id_type=MESH
        )

    near = (1, 3, 2)

    def row_at(d):
        return side + lax.rem(y + d, 4)

    def part(i, late):
        return pl.ds(KD, (i - 1) * B) if late else pl.ds(0, KD)

    def pivot_copy(i, n, late):
        cols = part(i, late)
        ss, rs = (qsend, qrecv) if late else (psend, precv)
        row = across if n == 0 else row_at(near[n - 1])
        return send(front_ref.at[0, :, cols], piv.at[i, :, cols], ss.at[n], rs.at[i], row=row)

    def pivot_pass(i, n, late):
        cols = part(i, late)
        ss, rs = (qsend, qrecv) if late else (psend, precv)
        return send(piv.at[i, :, cols], piv.at[i, :, cols], ss.at[4 + n], rs.at[i], row=row_at(near[n]))

    def pivot_own(i):
        cols = pl.ds(0, max(i + 1, 2) * B)
        return pltpu.make_async_copy(front_ref.at[0, :, cols], piv.at[i, :, cols], local.at[2])

    def pivot_hand(i, own, late):
        cols = part(i, late)
        ss, rs = (rsend, qrecv) if late else (fsend, precv)
        src = front_ref.at[0, :, cols] if own else piv.at[i, :, cols]
        return send(src, piv.at[i, :, cols], ss.at[i], rs.at[i], col=1)

    @pl.when(c == 0)
    def _():
        for late in (False, True):
            for i in range(2 if late else 0, R):
                @pl.when(r == i)
                def _():
                    for n in range(4):
                        pivot_copy(i, n, late).start()
                    pivot_hand(i, True, late).start()
                    if not late:
                        pivot_own(i).start()

    def hand_on(late):
        order = [across] + [row_at(d) for d in near] + [(4 - side) + lax.rem(y + d, 4) for d in near]
        for at, row in enumerate(order):
            for i in range(2 if late else 0, R):
                @pl.when(row == i)
                def _():
                    pivot_hand(i, False, late).wait_recv()
                    if at == 0:
                        for n in range(3):
                            pivot_pass(i, n, late).start()
                    pivot_hand(i, False, late).start()

    def contrib_panel(d, h):
        to = lax.rem(f + d, F)
        cols = pl.ds(h * PW, PW)
        return send(packed.at[to, :, cols], inc_p.at[f, :, cols], asend.at[h, d], arecv.at[h, d], front=to)

    def contrib_low(d):
        to = lax.rem(f + d, F)
        cols = pl.ds(PC, rest)
        return send(packed.at[to, :, cols], inc_ref.at[f, :, cols], bsend.at[d], brecv.at[d], front=to)

    def contrib_high(d):
        to = lax.rem(f + d, F)
        return send(packed.at[to], inc_ref.at[f], bsend.at[d], brecv.at[d], front=to)

    def place_copy(d):
        to = lax.rem(f + d, F)
        return send(place_v.at[to], got_ref.at[f], lsend.at[d], lrecv.at[d], front=to)

    def choice(to):
        which, place = 0, -1
        for k in range(4):
            mine = dest_ref[k] == to
            which = jnp.where(mine, k, which)
            place = jnp.where(mine, local_ref[k], place)
        return which, place

    load_contrib.wait()

    @pl.when(c == 0)
    def _():
        def one(d, carry):
            to = lax.rem(f + d, F)
            which, _ = choice(to)
            packed[to, :, :PC] = cont[which, :, :PC]
            return carry

        lax.fori_loop(1, F, one, 0)
        which, _ = choice(f)
        inc_p[f] = cont[which, :, :PC]

    def place_one(d, carry):
        to = lax.rem(f + d, F)
        _, place = choice(to)
        place_v[to] = jnp.full((8, B), place, jnp.int32)
        place_copy(d).start()
        return carry

    lax.fori_loop(1, F, place_one, 0)
    _, own_place = choice(f)
    got_ref[f] = jnp.full((8, B), own_place, jnp.int32)

    def pack_low(d, carry):
        to = lax.rem(f + d, F)
        which, _ = choice(to)
        packed[to, :, PC:] = cont[which, :, PC:]
        return carry

    def pack_high(d, carry):
        to = lax.rem(f + d, F)
        which, _ = choice(to)
        packed[to] = cont[which]
        return carry

    @pl.when(c == 0)
    def _():
        lax.fori_loop(0, F, pack_low, 0)

    @pl.when(c == 1)
    def _():
        lax.fori_loop(0, F, pack_high, 0)

    inc_own_low = pltpu.make_async_copy(packed.at[f, :, pl.ds(PC, rest)], inc_ref.at[f, :, pl.ds(PC, rest)], local.at[3])
    inc_own_high = pltpu.make_async_copy(packed.at[f], inc_ref.at[f], local.at[3])

    for d in range(1, F):
        place_copy(d).wait()

    @pl.when(c == 0)
    def _():
        hand_on(False)
        for d in range(1, F):
            contrib_panel(d, 0).start()
        for i in range(R):
            @pl.when(r == i)
            def _():
                pivot_own(i).wait()

    @pl.when(c == 1)
    def _():
        for i in range(R):
            pivot_hand(i, False, False).wait_recv()

    def half_of(h):
        return pl.ds(h * PW, PW)

    def own_second(n, h):
        cols = half_of(h)
        src, dst, ss, rs = pan.at[1, :, cols], win_ref.at[4 + r, :, cols], wsend.at[h, n], wrecv.at[h, 4 + r]
        if n == 0:
            return send(src, dst, ss, rs, row=across, col=1)
        if n == 1:
            return send(src, dst, ss, rs, col=1)
        return send(src, dst, ss, rs, row=row_at(near[n - 2]), col=1)

    def own_high(n, h):
        cols = half_of(h)
        src, dst, ss, rs = pan.at[0, :, cols], win_ref.at[r - 4, :, cols], wsend.at[h, 5 + n], wrecv.at[h, r - 4]
        if n == 0:
            return send(src, dst, ss, rs, row=across, col=1)
        if n == 1:
            return send(src, dst, ss, rs, col=1)
        return send(src, dst, ss, rs, row=row_at(near[n - 2]), col=1)

    def own_low(n, h):
        cols = half_of(h)
        src, dst, ss, rs = pan.at[0, :, cols], win_ref.at[r, :, cols], wsend.at[h, 5 + n], wrecv.at[h, r]
        if n == 0:
            return send(src, dst, ss, rs, row=across)
        return send(src, dst, ss, rs, row=row_at(near[n - 1]))

    keep_low = pltpu.make_async_copy(pan.at[0], win_ref.at[y], local.at[4])
    hand = send(pan, pan, hsend, hrecv, col=1)

    def landed(i, h):
        cols = half_of(h)
        return send(pan.at[0, :, cols], win_ref.at[i, :, cols], gsend.at[h, 0], wrecv.at[h, i], col=1 - c)

    def landed_all(i):
        for h in range(2):
            landed(i, h).wait_recv()

    def pass_second(n, h):
        here = win_ref.at[4 + across, :, half_of(h)]
        return send(here, here, gsend.at[h, n], wrecv.at[h, 4 + across], row=row_at(near[n]))

    def pass_first(n, h):
        here = win_ref.at[y, :, half_of(h)]
        return send(here, here, gsend.at[h, 3 + n], wrecv.at[h, y], row=row_at(near[n]))

    def assemble(lb, h):
        valid = (lb * R + r) * B < size_ref[0]
        cols = slice(h * PW, (h + 1) * PW)

        def eight(i, carry):
            at = pl.ds(pl.multiple_of(i * 8, 8), 8)
            total = jnp.where(valid, pan[lb - 1, at, cols], 0.0)
            for s in range(F):
                mask = jnp.concatenate([got_ref[s]] * (PW // B), 1) == lb
                total = total + jnp.where(mask, inc_p[s, at, cols], 0.0)
            pan[lb - 1, at, cols] = total
            return carry

        lax.fori_loop(0, B // 8, eight, 0)

    def after(k):
        @pl.when((k == 0) & (c == 0))
        def _():
            hand_on(True)
            for d in range(1, F):
                contrib_panel(d, 1).start()

        @pl.when((k == 1) & (c == 1))
        def _():
            for i in range(2, R):
                pivot_hand(i, False, True).wait_recv()

        for h in range(2):
            @pl.when((k == KA[h]) & (c == 0))
            def _():
                if h == 0:
                    load_panel.wait()
                for d in range(1, F):
                    contrib_panel(d, h).wait()
                assemble(2, h)
                for n in range(5):
                    own_second(n, h).start()
                assemble(1, h)

                @pl.when(r >= 4)
                def _():
                    for n in range(5):
                        own_high(n, h).start()

                @pl.when(r < 4)
                def _():
                    for n in range(4):
                        own_low(n, h).start()
                    if h == 1:
                        keep_low.start()

                if h == 1:
                    for d in range(1, F):
                        contrib_low(d).start()
                    inc_own_low.start()

                def others(lb, carry):
                    assemble(lb, h)
                    return carry

                lax.fori_loop(3, LB, others, 0)
                if h == 1:
                    hand.start()

        @pl.when((k == KC) & (c == 1))
        def _():
            for d in range(1, F):
                contrib_high(d).start()
            inc_own_high.start()

        for h in range(2):
            @pl.when((k == KF[h]) & (c == 0) & (r >= 4))
            def _():
                landed(y, h).wait_recv()
                for n in range(3):
                    pass_first(n, h).start()

            @pl.when((k == KF[h]) & (c == 1))
            def _():
                landed(4 + across, h).wait_recv()
                for n in range(3):
                    pass_second(n, h).start()

                @pl.when(r < 4)
                def _():
                    landed(y, h).wait_recv()
                    for n in range(3):
                        pass_first(n, h).start()

    cholesky_body(piv, l_ref, i_ref, x_ref, lh, ll, after)

    def solve(source, hi_ref, lo_ref, at, blocks):
        rows = slice(at * B, (at + blocks) * B)
        for k in range(PC // KD):
            o = k * KD
            cols = slice(o, o + KD)
            a = source[at : at + blocks, :, cols].reshape(blocks * B, KD)
            if k > 0:
                mine_h, mine_l = lh[cols, :o], ll[cols, :o]
                hi, lo = hi_ref[rows, :o], lo_ref[rows, :o]
                a = a - (dot_nt(hi, mine_h) + dot_nt(lo, mine_h) + dot_nt(hi, mine_l))
            hi_ref[rows, cols], lo_ref[rows, cols] = split(dot3(a, i_ref[k]))

    def out_copy(n, low):
        at = pl.ds(0, 4 * B) if low else pl.ds(0, 12 * B)
        pairs = ((ph, ph_ref), (plo, plo_ref), (wh.at[at], wh_ref.at[at]), (wl.at[at], wl_ref.at[at]))
        return pltpu.make_async_copy(*pairs[n], outs.at[n])

    @pl.when(c == 1)
    def _():
        hand.wait_recv()

    solve(pan, ph, plo, 0, 6)
    solve(pan, ph, plo, 6, 5)
    out_copy(0, False).start()
    out_copy(1, False).start()

    @pl.when(c == 0)
    def _():
        @pl.when(r < 4)
        def _():
            keep_low.wait()

        for i in range(4):
            @pl.when(y != i)
            def _():
                landed_all(i)

        solve(win_ref, wh, wl, 0, 4)
        out_copy(2, True).start()
        out_copy(3, True).start()

    @pl.when(c == 1)
    def _():
        for i in range(4):
            @pl.when((y != i) | (r >= 4))
            def _():
                landed_all(i)
        solve(win_ref, wh, wl, 0, 4)
        for half in range(2):
            for q in range(4 * half, 4 * half + 4):
                @pl.when(across != q)
                def _():
                    landed_all(4 + q)
            solve(win_ref, wh, wl, 4 * (half + 1), 4)
        out_copy(2, False).start()
        out_copy(3, False).start()

    @pl.when(c == 0)
    def _():
        for i in range(R):
            @pl.when(r == i)
            def _():
                for n in range(4):
                    pivot_copy(i, n, False).wait_send()
                    if i >= 2:
                        pivot_copy(i, n, True).wait_send()

            @pl.when(across == i)
            def _():
                for n in range(3):
                    pivot_pass(i, n, False).wait_send()
                    if i >= 2:
                        pivot_pass(i, n, True).wait_send()

            pivot_hand(i, False, False).wait_send()
            if i >= 2:
                pivot_hand(i, False, True).wait_send()
        for n in range(5):
            for h in range(2):
                own_second(n, h).wait_send()

        @pl.when(r >= 4)
        def _():
            for n in range(5):
                for h in range(2):
                    own_high(n, h).wait_send()
            for n in range(3):
                for h in range(2):
                    pass_first(n, h).wait_send()

        @pl.when(r < 4)
        def _():
            for n in range(4):
                for h in range(2):
                    own_low(n, h).wait_send()

        hand.wait_send()
        for d in range(1, F):
            contrib_low(d).wait()
        inc_own_low.wait()
        out_copy(2, True).wait()
        out_copy(3, True).wait()

    @pl.when(c == 1)
    def _():
        for n in range(3):
            for h in range(2):
                pass_second(n, h).wait_send()

        @pl.when(r < 4)
        def _():
            for n in range(3):
                for h in range(2):
                    pass_first(n, h).wait_send()

        for d in range(1, F):
            contrib_high(d).wait()
        inc_own_high.wait()
        out_copy(2, False).wait()
        out_copy(3, False).wait()

    out_copy(0, False).wait()
    out_copy(1, False).wait()


def exchange(front, contrib, dest, place, size):
    sm = pl.BlockSpec(memory_space=pltpu.SMEM)
    eight = pltpu.SemaphoreType.DMA((8,))
    one = pltpu.SemaphoreType.DMA
    own = ((LB - 1) * B, PC)
    window = (12 * B, PC)
    return pl.pallas_call(
        exchange_kernel,
        out_shape=(
            jax.ShapeDtypeStruct(own, BF16),
            jax.ShapeDtypeStruct(own, BF16),
            jax.ShapeDtypeStruct(window, BF16),
            jax.ShapeDtypeStruct(window, BF16),
            jax.ShapeDtypeStruct((F, B, HW), F32),
            jax.ShapeDtypeStruct((F, 8, B), jnp.int32),
            jax.ShapeDtypeStruct((PC, PC), F32),
        ),
        in_specs=[ANY, ANY, sm, sm, sm],
        out_specs=(ANY, ANY, ANY, ANY, ANY, VM, VM),
        scratch_shapes=[
            pltpu.VMEM((PC // KD, KD, KD), F32),
            pltpu.VMEM((NB, B, B), F32),
            pltpu.VMEM((PC, PC), BF16),
            pltpu.VMEM((PC, PC), BF16),
            pltpu.VMEM((4, B, HW), F32),
            pltpu.VMEM((F, B, HW), F32),
            pltpu.VMEM((LB - 1, B, PC), F32),
            pltpu.VMEM((12, B, PC), F32),
            pltpu.VMEM((F, B, PC), F32),
            pltpu.VMEM((R, B, PC), F32),
            pltpu.VMEM((F, 8, B), jnp.int32),
            pltpu.VMEM(own, BF16),
            pltpu.VMEM(own, BF16),
            pltpu.VMEM(window, BF16),
            pltpu.VMEM(window, BF16),
            eight,
            eight,
            eight,
            eight,
            eight,
            eight,
            pltpu.SemaphoreType.DMA((2, 8)),
            pltpu.SemaphoreType.DMA((2, 8)),
            eight,
            eight,
            eight,
            eight,
            one,
            one,
            pltpu.SemaphoreType.DMA((2, 10)),
            pltpu.SemaphoreType.DMA((2, 12)),
            pltpu.SemaphoreType.DMA((2, 6)),
            pltpu.SemaphoreType.DMA((6,)),
            pltpu.SemaphoreType.DMA((4,)),
        ],
        compiler_params=pltpu.CompilerParams(collective_id=0, has_side_effects=True, vmem_limit_bytes=62 * MIB),
    )(front, contrib, dest, place, size)


def final_kernel(meta_ref, front_ref, inc_ref, l_ref, ph, plo, wh, wl, out_ref):
    t = pl.program_id(0)
    col = meta_ref[1]
    steps = PC // KD

    @pl.when((col == 0) & (t < steps))
    def _():
        for k in range(steps):
            @pl.when(t == k)
            def _():
                cols = slice(k * KD, (k + 1) * KD)
                out_ref[0] = l_ref[:, cols]
                out_ref[1:] = (ph[:, cols].astype(F32) + plo[:, cols].astype(F32)).reshape(LB - 1, B, KD)

    @pl.when((col == 1) | (t >= steps))
    def _():
        start = pl.multiple_of((t - jnp.where(col == 0, steps, 0)) * KD, KD)
        w_hi, w_lo = wh[pl.ds(start, KD), :], wl[pl.ds(start, KD), :]
        update = dot_nt(ph[...], w_hi) + dot_nt(plo[...], w_hi) + dot_nt(ph[...], w_lo)
        out_ref[0] = jnp.zeros((B, KD), F32)
        for lb in range(1, LB):
            valid = (lb * R + meta_ref[0]) * B < meta_ref[2]
            out_ref[lb] = jnp.where(valid, front_ref[lb], 0.0) - update[(lb - 1) * B : lb * B]
        for s in range(F):
            place = meta_ref[3 + s]

            @pl.when(place >= 0)
            def _():
                out_ref[pl.ds(place, 1)] += inc_ref[s : s + 1]


def final(meta, front, inc, low, solved):
    tiles = HW // KD
    whole = dict(pipeline_mode=pl.Buffered(1))
    return pl.pallas_call(
        final_kernel,
        grid_spec=pltpu.PrefetchScalarGridSpec(
            num_scalar_prefetch=1,
            grid=(tiles,),
            in_specs=[
                pl.BlockSpec((LB, B, KD), lambda t, meta: (0, 0, t)),
                pl.BlockSpec((F, B, KD), lambda t, meta: (0, 0, t)),
                pl.BlockSpec((B, PC), lambda t, meta: (meta[0], 0), **whole),
                pl.BlockSpec(((LB - 1) * B, PC), lambda t, meta: (0, 0), **whole),
                pl.BlockSpec(((LB - 1) * B, PC), lambda t, meta: (0, 0), **whole),
                pl.BlockSpec((12 * B, PC), lambda t, meta: (0, 0), **whole),
                pl.BlockSpec((12 * B, PC), lambda t, meta: (0, 0), **whole),
            ],
            out_specs=pl.BlockSpec((LB, B, KD), lambda t, meta: (0, 0, t)),
        ),
        out_shape=jax.ShapeDtypeStruct((LB, B, HW), F32),
        compiler_params=pltpu.CompilerParams(vmem_limit_bytes=60 * MIB),
    )(meta, front, inc, low, *solved)


def on_device(front_matrix, front_sizes, contrib, dest_front, dest_local):
    front = front_matrix[0]
    *solved, inc, got, low = exchange(front, contrib[0], dest_front[0, :, 0], dest_local[0, :, 0], front_sizes)
    row_col = jnp.stack([lax.axis_index("row"), lax.axis_index("col"), front_sizes[0]]).astype(jnp.int32)
    meta = jnp.concatenate([row_col, got[:, 0, 0]])
    out = final(meta, front, inc, low, solved)
    return out[None]


def solution(mesh):
    return jax.shard_map(
        on_device,
        mesh=mesh,
        in_specs=(
            P("front", None, "row", "col"),
            P("front"),
            P("front", None, "row", "col"),
            P("front", None, "row"),
            P("front", None, "row"),
        ),
        out_specs=P("front", None, "row", "col"),
        check_vma=False,
    )
```

```python
import functools

import jax
import jax.numpy as jnp
from jax import lax
from jax.experimental import pallas as pl
from jax.experimental.pallas import tpu as pltpu
from jax.sharding import PartitionSpec as P

F = 8
R = 8
B = 128
LB = 12
HW = 1536
PC = 1024
NB = PC // B
PW = 512
KD = 256
KA = (1, 3)
KC = 5
KF = (3, 6)
MESH = pl.DeviceIdType.MESH
ANY = pl.BlockSpec(memory_space=pl.ANY)
VM = pl.BlockSpec(memory_space=pltpu.VMEM)
F32 = jnp.float32
BF16 = jnp.bfloat16
MIB = 2**20


def split(x):
    hi = x.astype(jnp.bfloat16)
    return hi, (x - hi.astype(F32)).astype(jnp.bfloat16)


def left3(hi, lo):
    return jnp.concatenate([hi, lo, hi], 1)


def right3(hi, lo):
    return jnp.concatenate([hi, hi, lo], 1)


def dot_nt(a, b):
    return lax.dot_general(a, b, (((1,), (1,)), ((), ())), preferred_element_type=F32)


def dot_nn(a, b):
    return lax.dot_general(a, b, (((1,), (0,)), ((), ())), preferred_element_type=F32)


def dot3(a, b):
    return dot_nt(left3(*split(a)), right3(*split(b)))


def dot3_nn(a, b):
    bh, bl = split(b)
    return dot_nn(left3(*split(a)), jnp.concatenate([bh, bh, bl], 0))


def recip(x):
    first = pl.reciprocal(x, approx=True)
    return first * (2.0 - x * first)


def lane_spread(x, k):
    return jnp.broadcast_to(x[:, k : k + 1], (8, B))


def row_spread(x, j):
    return jnp.broadcast_to(x[j : j + 1, :], (8, B))


def factor_block(sym):
    sub = lax.broadcasted_iota(jnp.int32, (8, B), 0)
    lane = lax.broadcasted_iota(jnp.int32, (8, B), 1)
    count = B // 8
    rows = [sym[q * 8 : (q + 1) * 8, :] for q in range(count)]
    eyes = [jnp.where(lane == sub + q * 8, 1.0, 0.0).astype(F32) for q in range(count)]
    factor, inverse = [], []
    for p in range(count):
        v, e = rows[p], eyes[p]
        c = [lane_spread(v, p * 8 + k) for k in range(8)]
        more = p < count - 1
        if more:
            v2, e2 = rows[p + 1], eyes[p + 1]
            c2 = [lane_spread(v2, p * 8 + k) for k in range(8)]
        diagonal = None
        for j in range(8):
            pivot = row_spread(c[j], j)
            diagonal = pivot if diagonal is None else jnp.where(sub == j, pivot, diagonal)
            over = recip(pivot)
            rv, re = row_spread(v, j), row_spread(e, j)
            m = jnp.where(sub > j, c[j] * over, 0.0)
            if more:
                m2 = c2[j] * over
            for k in range(j + 1, 8):
                s = row_spread(c[k], j)
                c[k] = c[k] - m * s
                if more:
                    c2[k] = c2[k] - m2 * s
            v = v - m * rv
            e = e - m * re
            if more:
                v2 = v2 - m2 * rv
                e2 = e2 - m2 * re
        scale = lax.rsqrt(diagonal)
        factor.append(jnp.where(lane >= sub + p * 8, v * scale, 0.0))
        inverse.append(e * scale)
        if more:
            rows[p + 1], eyes[p + 1] = v2, e2
        if p < count - 2:
            t = (v * recip(diagonal)).T
            rv = [row_spread(v, j) for j in range(8)]
            re = [row_spread(e, j) for j in range(8)]
            for q in range(p + 2, count):
                tq = t[q * 8 : (q + 1) * 8, :]
                for j in range(8):
                    m = jnp.broadcast_to(tq[:, j : j + 1], (8, B))
                    rows[q] = rows[q] - m * rv[j]
                    eyes[q] = eyes[q] - m * re[j]
    return jnp.concatenate(factor, 0), jnp.concatenate(inverse, 0)


def cholesky_body(a_ref, l_ref, i_ref, x_ref, lh, ll, after):
    row_id = lax.broadcasted_iota(jnp.int32, (B, B), 0)
    col_id = lax.broadcasted_iota(jnp.int32, (B, B), 1)

    def step(k, carry):
        def owed(kk):
            def run():
                o = kk * B
                a = a_ref[kk:, :, o : o + B].reshape(PC - o, B)
                if kk > 0:
                    mine_h, mine_l = lh[o : o + B, :o], ll[o : o + B, :o]
                    a = a - (dot_nt(lh[o:, :o], mine_h) + dot_nt(ll[o:, :o], mine_h) + dot_nt(lh[o:, :o], mine_l))
                l_ref[o:, o : o + B] = a

            return run

        for kk in range(NB):
            pl.when(k == kk)(owed(kk))
        o = pl.multiple_of(k * B, B)
        d = l_ref[pl.ds(o, B), pl.ds(o, B)]
        lt, li = factor_block(jnp.where(row_id >= col_id, d, d.T))
        l_ref[pl.ds(o, B), pl.ds(o, B)] = lt.T
        x_ref[k] = li

        def below(kk):
            def run():
                base = (kk + 1) * B
                x = dot3(l_ref[base:, kk * B : base], li)
                l_ref[base:, kk * B : base] = x
                lh[base:, kk * B : base], ll[base:, kk * B : base] = split(x)

            return run

        for kk in range(NB - 1):
            pl.when(k == kk)(below(kk))
        after(k)
        return carry

    lax.fori_loop(0, NB, step, 0)
    for i in range(NB - 1):
        l_ref[i * B : (i + 1) * B, (i + 1) * B :] = jnp.zeros((B, (NB - 1 - i) * B), F32)
    for i in range(NB // 2):
        low, high = x_ref[2 * i], x_ref[2 * i + 1]
        between = l_ref[(2 * i + 1) * B : (2 * i + 2) * B, 2 * i * B : (2 * i + 1) * B]
        i_ref[i, :B, :B] = low
        i_ref[i, :B, B:] = jnp.zeros((B, B), F32)
        i_ref[i, B:, :B] = -dot3_nn(high, dot3_nn(between, low))
        i_ref[i, B:, B:] = high


def exchange_kernel(
    front_ref, contrib_ref, dest_ref, local_ref, size_ref,
    ph_ref, plo_ref, wh_ref, wl_ref, inc_ref, got_ref, l_ref,
    i_ref, x_ref, lh, ll, cont, packed, pan, win_ref, inc_p, piv, place_v, ph, plo, wh, wl,
    psend, precv, fsend, qsend, qrecv, rsend, asend, arecv, bsend, brecv, lsend, lrecv, hsend, hrecv, wsend, wrecv, gsend, local, outs,
):
    f = lax.axis_index("front")
    r = lax.axis_index("row")
    c = lax.axis_index("col")
    y = lax.rem(r, 4)
    side = r - y
    across = lax.rem(r + 4, R)
    rest = HW - PC

    load_contrib = pltpu.make_async_copy(contrib_ref, cont, local.at[0])
    load_contrib.start()
    load_panel = pltpu.make_async_copy(front_ref.at[pl.ds(1, LB - 1), :, pl.ds(0, PC)], pan, local.at[1])

    @pl.when(c == 0)
    def _():
        load_panel.start()

    barrier = pltpu.get_barrier_semaphore()
    for d in range(1, F):
        pl.semaphore_signal(barrier, inc=1, device_id={"front": lax.rem(f + d, F)}, device_id_type=MESH)
        pl.semaphore_signal(barrier, inc=1, device_id={"row": lax.rem(r + d, R)}, device_id_type=MESH)
    for d in range(R):
        pl.semaphore_signal(barrier, inc=1, device_id={"row": lax.rem(r + d, R), "col": 1 - c}, device_id_type=MESH)
    pl.semaphore_wait(barrier, F - 1 + R - 1 + R)

    def send(src, dst, send_sem, recv_sem, **device):
        return pltpu.make_async_remote_copy(
            src_ref=src, dst_ref=dst, send_sem=send_sem, recv_sem=recv_sem, device_id=device, device_id_type=MESH
        )

    near = (1, 3, 2)

    def row_at(d):
        return side + lax.rem(y + d, 4)

    def part(i, late):
        return pl.ds(KD, (i - 1) * B) if late else pl.ds(0, KD)

    def pivot_copy(i, n, late):
        cols = part(i, late)
        ss, rs = (qsend, qrecv) if late else (psend, precv)
        row = across if n == 0 else row_at(near[n - 1])
        return send(front_ref.at[0, :, cols], piv.at[i, :, cols], ss.at[n], rs.at[i], row=row)

    def pivot_pass(i, n, late):
        cols = part(i, late)
        ss, rs = (qsend, qrecv) if late else (psend, precv)
        return send(piv.at[i, :, cols], piv.at[i, :, cols], ss.at[4 + n], rs.at[i], row=row_at(near[n]))

    def pivot_own(i):
        cols = pl.ds(0, max(i + 1, 2) * B)
        return pltpu.make_async_copy(front_ref.at[0, :, cols], piv.at[i, :, cols], local.at[2])

    def pivot_hand(i, own, late):
        cols = part(i, late)
        ss, rs = (rsend, qrecv) if late else (fsend, precv)
        src = front_ref.at[0, :, cols] if own else piv.at[i, :, cols]
        return send(src, piv.at[i, :, cols], ss.at[i], rs.at[i], col=1)

    @pl.when(c == 0)
    def _():
        for late in (False, True):
            for i in range(2 if late else 0, R):
                @pl.when(r == i)
                def _():
                    for n in range(4):
                        pivot_copy(i, n, late).start()
                    pivot_hand(i, True, late).start()
                    if not late:
                        pivot_own(i).start()

    def hand_on(late):
        order = [across] + [row_at(d) for d in near] + [(4 - side) + lax.rem(y + d, 4) for d in near]
        for at, row in enumerate(order):
            for i in range(2 if late else 0, R):
                @pl.when(row == i)
                def _():
                    pivot_hand(i, False, late).wait_recv()
                    if at == 0:
                        for n in range(3):
                            pivot_pass(i, n, late).start()
                    pivot_hand(i, False, late).start()

    def contrib_panel(d, h):
        to = lax.rem(f + d, F)
        cols = pl.ds(h * PW, PW)
        return send(packed.at[to, :, cols], inc_p.at[f, :, cols], asend.at[h, d], arecv.at[h, d], front=to)

    def contrib_low(d):
        to = lax.rem(f + d, F)
        cols = pl.ds(PC, rest)
        return send(packed.at[to, :, cols], inc_ref.at[f, :, cols], bsend.at[d], brecv.at[d], front=to)

    def contrib_high(d):
        to = lax.rem(f + d, F)
        return send(packed.at[to], inc_ref.at[f], bsend.at[d], brecv.at[d], front=to)

    def place_copy(d):
        to = lax.rem(f + d, F)
        return send(place_v.at[to], got_ref.at[f], lsend.at[d], lrecv.at[d], front=to)

    def choice(to):
        which, place = 0, -1
        for k in range(4):
            mine = dest_ref[k] == to
            which = jnp.where(mine, k, which)
            place = jnp.where(mine, local_ref[k], place)
        return which, place

    load_contrib.wait()

    @pl.when(c == 0)
    def _():
        def one(d, carry):
            to = lax.rem(f + d, F)
            which, _ = choice(to)
            packed[to, :, :PC] = cont[which, :, :PC]
            return carry

        lax.fori_loop(1, F, one, 0)
        which, _ = choice(f)
        inc_p[f] = cont[which, :, :PC]

    def place_one(d, carry):
        to = lax.rem(f + d, F)
        _, place = choice(to)
        place_v[to] = jnp.full((8, B), place, jnp.int32)
        place_copy(d).start()
        return carry

    lax.fori_loop(1, F, place_one, 0)
    _, own_place = choice(f)
    got_ref[f] = jnp.full((8, B), own_place, jnp.int32)

    def pack_low(d, carry):
        to = lax.rem(f + d, F)
        which, _ = choice(to)
        packed[to, :, PC:] = cont[which, :, PC:]
        return carry

    def pack_high(d, carry):
        to = lax.rem(f + d, F)
        which, _ = choice(to)
        packed[to] = cont[which]
        return carry

    @pl.when(c == 0)
    def _():
        lax.fori_loop(0, F, pack_low, 0)

    @pl.when(c == 1)
    def _():
        lax.fori_loop(0, F, pack_high, 0)

    inc_own_low = pltpu.make_async_copy(packed.at[f, :, pl.ds(PC, rest)], inc_ref.at[f, :, pl.ds(PC, rest)], local.at[3])
    inc_own_high = pltpu.make_async_copy(packed.at[f], inc_ref.at[f], local.at[3])

    for d in range(1, F):
        place_copy(d).wait()

    @pl.when(c == 0)
    def _():
        hand_on(False)
        for d in range(1, F):
            contrib_panel(d, 0).start()
        for i in range(R):
            @pl.when(r == i)
            def _():
                pivot_own(i).wait()

    @pl.when(c == 1)
    def _():
        for i in range(R):
            pivot_hand(i, False, False).wait_recv()

    def half_of(h):
        return pl.ds(h * PW, PW)

    def own_second(n, h):
        cols = half_of(h)
        src, dst, ss, rs = pan.at[1, :, cols], win_ref.at[4 + r, :, cols], wsend.at[h, n], wrecv.at[h, 4 + r]
        if n == 0:
            return send(src, dst, ss, rs, row=across, col=1)
        if n == 1:
            return send(src, dst, ss, rs, col=1)
        return send(src, dst, ss, rs, row=row_at(near[n - 2]), col=1)

    def own_high(n, h):
        cols = half_of(h)
        src, dst, ss, rs = pan.at[0, :, cols], win_ref.at[r - 4, :, cols], wsend.at[h, 5 + n], wrecv.at[h, r - 4]
        if n == 0:
            return send(src, dst, ss, rs, row=across, col=1)
        if n == 1:
            return send(src, dst, ss, rs, col=1)
        return send(src, dst, ss, rs, row=row_at(near[n - 2]), col=1)

    def own_low(n, h):
        cols = half_of(h)
        src, dst, ss, rs = pan.at[0, :, cols], win_ref.at[r, :, cols], wsend.at[h, 5 + n], wrecv.at[h, r]
        if n == 0:
            return send(src, dst, ss, rs, row=across)
        return send(src, dst, ss, rs, row=row_at(near[n - 1]))

    keep_low = pltpu.make_async_copy(pan.at[0], win_ref.at[y], local.at[4])
    hand = send(pan, pan, hsend, hrecv, col=1)

    def landed(i, h):
        cols = half_of(h)
        return send(pan.at[0, :, cols], win_ref.at[i, :, cols], gsend.at[h, 0], wrecv.at[h, i], col=1 - c)

    def landed_all(i):
        for h in range(2):
            landed(i, h).wait_recv()

    def pass_second(n, h):
        here = win_ref.at[4 + across, :, half_of(h)]
        return send(here, here, gsend.at[h, n], wrecv.at[h, 4 + across], row=row_at(near[n]))

    def pass_first(n, h):
        here = win_ref.at[y, :, half_of(h)]
        return send(here, here, gsend.at[h, 3 + n], wrecv.at[h, y], row=row_at(near[n]))

    def assemble(lb, h):
        valid = (lb * R + r) * B < size_ref[0]
        cols = slice(h * PW, (h + 1) * PW)

        def eight(i, carry):
            at = pl.ds(pl.multiple_of(i * 8, 8), 8)
            total = jnp.where(valid, pan[lb - 1, at, cols], 0.0)
            for s in range(F):
                mask = jnp.concatenate([got_ref[s]] * (PW // B), 1) == lb
                total = total + jnp.where(mask, inc_p[s, at, cols], 0.0)
            pan[lb - 1, at, cols] = total
            return carry

        lax.fori_loop(0, B // 8, eight, 0)

    def after(k):
        @pl.when((k == 0) & (c == 0))
        def _():
            hand_on(True)
            for d in range(1, F):
                contrib_panel(d, 1).start()

        @pl.when((k == 1) & (c == 1))
        def _():
            for i in range(2, R):
                pivot_hand(i, False, True).wait_recv()

        for h in range(2):
            @pl.when((k == KA[h]) & (c == 0))
            def _():
                if h == 0:
                    load_panel.wait()
                for d in range(1, F):
                    contrib_panel(d, h).wait()
                assemble(2, h)
                for n in range(5):
                    own_second(n, h).start()
                assemble(1, h)

                @pl.when(r >= 4)
                def _():
                    for n in range(5):
                        own_high(n, h).start()

                @pl.when(r < 4)
                def _():
                    for n in range(4):
                        own_low(n, h).start()
                    if h == 1:
                        keep_low.start()

                if h == 1:
                    for d in range(1, F):
                        contrib_low(d).start()
                    inc_own_low.start()

                def others(lb, carry):
                    assemble(lb, h)
                    return carry

                lax.fori_loop(3, LB, others, 0)
                if h == 1:
                    hand.start()

        @pl.when((k == KC) & (c == 1))
        def _():
            for d in range(1, F):
                contrib_high(d).start()
            inc_own_high.start()

        for h in range(2):
            @pl.when((k == KF[h]) & (c == 0) & (r >= 4))
            def _():
                landed(y, h).wait_recv()
                for n in range(3):
                    pass_first(n, h).start()

            @pl.when((k == KF[h]) & (c == 1))
            def _():
                landed(4 + across, h).wait_recv()
                for n in range(3):
                    pass_second(n, h).start()

                @pl.when(r < 4)
                def _():
                    landed(y, h).wait_recv()
                    for n in range(3):
                        pass_first(n, h).start()

    cholesky_body(piv, l_ref, i_ref, x_ref, lh, ll, after)

    def solve(source, hi_ref, lo_ref, at, blocks):
        rows = slice(at * B, (at + blocks) * B)
        for k in range(PC // KD):
            o = k * KD
            cols = slice(o, o + KD)
            a = source[at : at + blocks, :, cols].reshape(blocks * B, KD)
            if k > 0:
                mine_h, mine_l = lh[cols, :o], ll[cols, :o]
                hi, lo = hi_ref[rows, :o], lo_ref[rows, :o]
                a = a - (dot_nt(hi, mine_h) + dot_nt(lo, mine_h) + dot_nt(hi, mine_l))
            hi_ref[rows, cols], lo_ref[rows, cols] = split(dot3(a, i_ref[k]))

    def out_copy(n, low):
        at = pl.ds(0, 4 * B) if low else pl.ds(0, 12 * B)
        pairs = ((ph, ph_ref), (plo, plo_ref), (wh.at[at], wh_ref.at[at]), (wl.at[at], wl_ref.at[at]))
        return pltpu.make_async_copy(*pairs[n], outs.at[n])

    @pl.when(c == 1)
    def _():
        hand.wait_recv()

    solve(pan, ph, plo, 0, 6)
    solve(pan, ph, plo, 6, 5)
    out_copy(0, False).start()
    out_copy(1, False).start()

    @pl.when(c == 0)
    def _():
        @pl.when(r < 4)
        def _():
            keep_low.wait()

        for i in range(4):
            @pl.when(y != i)
            def _():
                landed_all(i)

        solve(win_ref, wh, wl, 0, 4)
        out_copy(2, True).start()
        out_copy(3, True).start()

    @pl.when(c == 1)
    def _():
        for i in range(4):
            @pl.when((y != i) | (r >= 4))
            def _():
                landed_all(i)
        solve(win_ref, wh, wl, 0, 4)
        for half in range(2):
            for q in range(4 * half, 4 * half + 4):
                @pl.when(across != q)
                def _():
                    landed_all(4 + q)
            solve(win_ref, wh, wl, 4 * (half + 1), 4)
        out_copy(2, False).start()
        out_copy(3, False).start()

    @pl.when(c == 0)
    def _():
        for i in range(R):
            @pl.when(r == i)
            def _():
                for n in range(4):
                    pivot_copy(i, n, False).wait_send()
                    if i >= 2:
                        pivot_copy(i, n, True).wait_send()

            @pl.when(across == i)
            def _():
                for n in range(3):
                    pivot_pass(i, n, False).wait_send()
                    if i >= 2:
                        pivot_pass(i, n, True).wait_send()

            pivot_hand(i, False, False).wait_send()
            if i >= 2:
                pivot_hand(i, False, True).wait_send()
        for n in range(5):
            for h in range(2):
                own_second(n, h).wait_send()

        @pl.when(r >= 4)
        def _():
            for n in range(5):
                for h in range(2):
                    own_high(n, h).wait_send()
            for n in range(3):
                for h in range(2):
                    pass_first(n, h).wait_send()

        @pl.when(r < 4)
        def _():
            for n in range(4):
                for h in range(2):
                    own_low(n, h).wait_send()

        hand.wait_send()
        for d in range(1, F):
            contrib_low(d).wait()
        inc_own_low.wait()
        out_copy(2, True).wait()
        out_copy(3, True).wait()

    @pl.when(c == 1)
    def _():
        for n in range(3):
            for h in range(2):
                pass_second(n, h).wait_send()

        @pl.when(r < 4)
        def _():
            for n in range(3):
                for h in range(2):
                    pass_first(n, h).wait_send()

        for d in range(1, F):
            contrib_high(d).wait()
        inc_own_high.wait()
        out_copy(2, False).wait()
        out_copy(3, False).wait()

    out_copy(0, False).wait()
    out_copy(1, False).wait()


def exchange(front, contrib, dest, place, size):
    sm = pl.BlockSpec(memory_space=pltpu.SMEM)
    eight = pltpu.SemaphoreType.DMA((8,))
    one = pltpu.SemaphoreType.DMA
    own = ((LB - 1) * B, PC)
    window = (12 * B, PC)
    return pl.pallas_call(
        exchange_kernel,
        out_shape=(
            jax.ShapeDtypeStruct(own, BF16),
            jax.ShapeDtypeStruct(own, BF16),
            jax.ShapeDtypeStruct(window, BF16),
            jax.ShapeDtypeStruct(window, BF16),
            jax.ShapeDtypeStruct((F, B, HW), F32),
            jax.ShapeDtypeStruct((F, 8, B), jnp.int32),
            jax.ShapeDtypeStruct((PC, PC), F32),
        ),
        in_specs=[ANY, ANY, sm, sm, sm],
        out_specs=(ANY, ANY, ANY, ANY, ANY, VM, VM),
        scratch_shapes=[
            pltpu.VMEM((PC // KD, KD, KD), F32),
            pltpu.VMEM((NB, B, B), F32),
            pltpu.VMEM((PC, PC), BF16),
            pltpu.VMEM((PC, PC), BF16),
            pltpu.VMEM((4, B, HW), F32),
            pltpu.VMEM((F, B, HW), F32),
            pltpu.VMEM((LB - 1, B, PC), F32),
            pltpu.VMEM((12, B, PC), F32),
            pltpu.VMEM((F, B, PC), F32),
            pltpu.VMEM((R, B, PC), F32),
            pltpu.VMEM((F, 8, B), jnp.int32),
            pltpu.VMEM(own, BF16),
            pltpu.VMEM(own, BF16),
            pltpu.VMEM(window, BF16),
            pltpu.VMEM(window, BF16),
            eight,
            eight,
            eight,
            eight,
            eight,
            eight,
            pltpu.SemaphoreType.DMA((2, 8)),
            pltpu.SemaphoreType.DMA((2, 8)),
            eight,
            eight,
            eight,
            eight,
            one,
            one,
            pltpu.SemaphoreType.DMA((2, 10)),
            pltpu.SemaphoreType.DMA((2, 12)),
            pltpu.SemaphoreType.DMA((2, 6)),
            pltpu.SemaphoreType.DMA((6,)),
            pltpu.SemaphoreType.DMA((4,)),
        ],
        compiler_params=pltpu.CompilerParams(collective_id=0, has_side_effects=True, vmem_limit_bytes=62 * MIB),
    )(front, contrib, dest, place, size)


def final_kernel(meta_ref, front_ref, inc_ref, l_ref, ph, plo, wh, wl, out_ref):
    t = pl.program_id(0)
    col = meta_ref[1]
    steps = PC // KD

    @pl.when((col == 0) & (t < steps))
    def _():
        for k in range(steps):
            @pl.when(t == k)
            def _():
                cols = slice(k * KD, (k + 1) * KD)
                out_ref[0] = l_ref[:, cols]
                out_ref[1:] = (ph[:, cols].astype(F32) + plo[:, cols].astype(F32)).reshape(LB - 1, B, KD)

    @pl.when((col == 1) | (t >= steps))
    def _():
        start = pl.multiple_of((t - jnp.where(col == 0, steps, 0)) * KD, KD)
        w_hi, w_lo = wh[pl.ds(start, KD), :], wl[pl.ds(start, KD), :]
        update = dot_nt(ph[...], w_hi) + dot_nt(plo[...], w_hi) + dot_nt(ph[...], w_lo)
        out_ref[0] = jnp.zeros((B, KD), F32)
        for lb in range(1, LB):
            valid = (lb * R + meta_ref[0]) * B < meta_ref[2]
            out_ref[lb] = jnp.where(valid, front_ref[lb], 0.0) - update[(lb - 1) * B : lb * B]
        for s in range(F):
            place = meta_ref[3 + s]

            @pl.when(place >= 0)
            def _():
                out_ref[pl.ds(place, 1)] += inc_ref[s : s + 1]


def final(meta, front, inc, low, solved):
    tiles = HW // KD
    whole = dict(pipeline_mode=pl.Buffered(1))
    return pl.pallas_call(
        final_kernel,
        grid_spec=pltpu.PrefetchScalarGridSpec(
            num_scalar_prefetch=1,
            grid=(tiles,),
            in_specs=[
                pl.BlockSpec((LB, B, KD), lambda t, meta: (0, 0, t)),
                pl.BlockSpec((F, B, KD), lambda t, meta: (0, 0, t)),
                pl.BlockSpec((B, PC), lambda t, meta: (meta[0], 0), **whole),
                pl.BlockSpec(((LB - 1) * B, PC), lambda t, meta: (0, 0), **whole),
                pl.BlockSpec(((LB - 1) * B, PC), lambda t, meta: (0, 0), **whole),
                pl.BlockSpec((12 * B, PC), lambda t, meta: (0, 0), **whole),
                pl.BlockSpec((12 * B, PC), lambda t, meta: (0, 0), **whole),
            ],
            out_specs=pl.BlockSpec((LB, B, KD), lambda t, meta: (0, 0, t)),
        ),
        out_shape=jax.ShapeDtypeStruct((LB, B, HW), F32),
        compiler_params=pltpu.CompilerParams(vmem_limit_bytes=60 * MIB),
    )(meta, front, inc, low, *solved)


def on_device(front_matrix, front_sizes, contrib, dest_front, dest_local):
    front = front_matrix[0]
    *solved, inc, got, low = exchange(front, contrib[0], dest_front[0, :, 0], dest_local[0, :, 0], front_sizes)
    row_col = jnp.stack([lax.axis_index("row"), lax.axis_index("col"), front_sizes[0]]).astype(jnp.int32)
    meta = jnp.concatenate([row_col, got[:, 0, 0]])
    out = final(meta, front, inc, low, solved)
    return out[None]


def solution(mesh):
    return jax.shard_map(
        on_device,
        mesh=mesh,
        in_specs=(
            P("front", None, "row", "col"),
            P("front"),
            P("front", None, "row", "col"),
            P("front", None, "row"),
            P("front", None, "row"),
        ),
        out_specs=P("front", None, "row", "col"),
        check_vma=False,
    )
```
